128 devices in a mesh: dp: 8 (over y, core), fsdp: 16 (over z, x).
Axes of the slice: x: 4, y: 4, z: 4, core: 2. Of those that a mesh axis runs over, the one named last changes fastest.
Arguments:
- waveforms: bfloat16 [8, 2048, 320], P('dp', 'fsdp'), may hold values from -6 to 6
- packing_list: int32 [4, 2048], P(None, 'fsdp'), may hold values from 0 to 128, as said below
- segment_ids: int32 [8, 2048], P('dp', 'fsdp'), may hold values from -1 to 127, as said below
- first_weight: bfloat16 [512, 10], P('fsdp'), may hold values from -2 to 2
- first_bias: bfloat16 [512], P('fsdp'), may hold values from -3 to 3
- first_gain: bfloat16 [512], P('fsdp'), may hold values from 0.5 to 1.5
- first_shift: bfloat16 [512], P('fsdp'), may hold values from -3 to 3
- second_weight: bfloat16 [512, 1536], P('fsdp'), may hold values from -0.15625 to 0.15625
- second_bias: bfloat16 [512], P('fsdp'), may hold values from -3 to 3
- second_gain: bfloat16 [512], P('fsdp'), may hold values from 0.5 to 1.5
- second_shift: bfloat16 [512], P('fsdp'), may hold values from -3 to 3
- cotangent: bfloat16 [8, 65536, 512], P('dp', 'fsdp'), may hold values from -0.01171875 to 0.01171875
Outputs:
- features: bfloat16 [8, 65536, 512], P('dp', 'fsdp')
- first_weight_grad: float32 [512, 10], P('fsdp')
- first_bias_grad: float32 [512], P('fsdp')
- first_gain_grad: float32 [512], P('fsdp')
- first_shift_grad: float32 [512], P('fsdp')
- second_weight_grad: float32 [512, 1536], P('fsdp')
- second_bias_grad: float32 [512], P('fsdp')
- second_gain_grad: float32 [512], P('fsdp')
- second_shift_grad: float32 [512], P('fsdp')
The draws below stay inside these ranges and needn't reach their ends.
Inputs may be any that keep to these rules, and one draw needn't show every extreme that they name: `packing_list`: columns j * 128 to (j + 1) * 128 - 1 are the list of fsdp index j, the same for every dp index. Rows: source reader (a dp index), owner (a dp index), frame offset in the owner's packed sequence, length in frames (0 for an empty entry, whose offset is 128). Entries come two for each (reader, owner) pair, in shuffled order. A reader sends at most 16 frames to one owner; in every column one reader sends exactly 16 frames to every owner and one owner receives exactly 16 frames from every reader. An owner's utterances do not intersect and end within its 128 frames. `segment_ids`: the list index of the utterance covering each frame of an owner's packed sequence, -1 where none does.
All inputs are finite; a program needn't handle non-finite values.
Results may differ from the reference program's by a relative error of at most 0.0055.
Values may be sent and summed in bfloat16 or wider, within the bound.
A program may use at most 256 MiB of HBM per device.

```python
from functools import partial
import jax
import jax.numpy as jnp
from jax import lax

CH = 512
PACK_FR = 128
SLOT_FR = 16
LIST = 128
POS1 = 4096
N_DP = 8
N_FSDP = 16


def column_plan(key):
    keys = jax.random.split(key, 6)
    pairs = N_DP * N_DP
    pair_index = jnp.arange(pairs, dtype=jnp.int32)
    reader = pair_index // N_DP
    target = pair_index % N_DP
    totals = jax.random.randint(keys[0], (pairs,), 0, SLOT_FR + 1, dtype=jnp.int32)
    busy_owner = jax.random.randint(keys[1], (), 0, N_DP, dtype=jnp.int32)
    busy_reader = jax.random.randint(keys[2], (), 0, N_DP, dtype=jnp.int32)
    light_owner = (busy_owner + 1) % N_DP
    light_reader = (busy_reader + 1) % N_DP
    busy_pair = (reader == busy_reader) & (target == busy_owner)
    totals = jnp.where((target == light_owner) & (reader == light_reader), 0, totals)
    totals = jnp.where((target == busy_owner) | (reader == busy_reader), SLOT_FR, totals).astype(jnp.int32)
    first_part = jax.random.randint(keys[3], (pairs,), 0, totals + 1, dtype=jnp.int32)
    first_part = jnp.where(busy_pair, 0, first_part).astype(jnp.int32)
    lengths = jnp.stack([first_part, totals - first_part], axis=1).reshape(LIST)
    sources = jnp.repeat(reader, 2)
    owners = jnp.repeat(target, 2)
    shuffle = jax.random.permutation(keys[4], LIST).astype(jnp.int32)
    last_entry = (2 * (busy_reader * N_DP + busy_owner) + 1).astype(jnp.int32)
    where_last = jnp.argmax((shuffle == last_entry).astype(jnp.int32))
    shuffle = shuffle.at[where_last].set(shuffle[LIST - 1]).at[LIST - 1].set(last_entry)
    lengths = lengths[shuffle]
    sources = sources[shuffle]
    owners = owners[shuffle]
    ranking = jax.random.permutation(keys[5], LIST)
    same_owner = owners[None, :] == owners[:, None]
    before = ranking[None, :] < ranking[:, None]
    offsets = jnp.sum(jnp.where(same_owner & before, lengths[None, :], 0), axis=1).astype(jnp.int32)
    offsets = jnp.where(lengths == 0, PACK_FR, offsets).astype(jnp.int32)
    frame_index = jnp.arange(PACK_FR, dtype=jnp.int32)
    owner_index = jnp.arange(N_DP, dtype=jnp.int32)
    covered = (owners[None, None, :] == owner_index[:, None, None]) & (frame_index[None, :, None] >= offsets[None, None, :]) & (frame_index[None, :, None] < (offsets + lengths)[None, None, :])
    entry_ids = jnp.arange(LIST, dtype=jnp.int32)
    segments = jnp.where(jnp.any(covered, axis=2), jnp.sum(jnp.where(covered, entry_ids, 0), axis=2), -1)
    table = jnp.stack([sources, owners, offsets, lengths]).astype(jnp.int32)
    return (table, segments.astype(jnp.int32))


def packing_plan(key):
    keys = jax.random.split(key, N_FSDP)
    tables, segments = jax.vmap(column_plan)(keys)
    table = jnp.transpose(tables, (1, 0, 2)).reshape(4, N_FSDP * LIST)
    segment_table = jnp.transpose(segments, (1, 0, 2)).reshape(N_DP, N_FSDP * PACK_FR)
    return (table, segment_table)


def draw_packing_list(key, part):
    return packing_plan(key)[0]


def draw_segment_ids(key, part):
    return packing_plan(key)[1]


def with_spikes(array, rng, source, target, blocks, factor):
    def block_of(axis_at):
        return (jnp.arange(array.shape[axis_at]) // (array.shape[axis_at] // blocks)).reshape((-1,) + (1,) * (array.ndim - 1 - axis_at))

    one_side = jax.random.permutation(rng, blocks)[block_of(target)]
    far = (block_of(target) + blocks // 2) % blocks
    return jnp.where((block_of(source) == one_side) | (block_of(source) == far), factor * array, array)


def block_scale(key, dims, cuts, low, top_value):
    def one(dim, parts):
        steps = jax.random.uniform(jax.random.fold_in(jax.random.fold_in(key, 6), dim), (parts,), jnp.float32, low / len(cuts), top_value / len(cuts))
        return jnp.repeat(jnp.exp(steps), dims[dim] // parts).reshape((-1,) + (1,) * (len(dims) - dim - 1))

    gain = one(*cuts[0])
    for cut in cuts[1:]:
        gain = gain * one(*cut)
    return gain


def noise(key, dims, scale, limit, cuts=(), kind=jnp.bfloat16):
    values = scale * jax.random.normal(key, dims, jnp.float32)
    if cuts:
        values = values * block_scale(key, dims, cuts, -0.22, 0.18)
    return jnp.clip(values, -limit, limit).astype(kind)


def bell_draw_with(rng, extent, scale, limit, cuts, heavy, kind=jnp.bfloat16):
    result = scale * jax.random.normal(rng, extent, jnp.float32)
    if cuts:
        result = result * block_scale(rng, extent, cuts, -0.22, 0.18)
    return jnp.clip(with_spikes(result, jax.random.fold_in(rng, 3), *heavy), -limit, limit).astype(kind)


def setup_inputs(seed: int = 0) -> dict:
    key_of = jax.random.split(jax.random.key(seed), 13)
    waveforms = noise(key_of[0], (N_DP, N_FSDP * PACK_FR, 320), 1.0, 6.0, ((0, 8), (1, 16)))
    packing_list = draw_packing_list(jax.random.fold_in(key_of[12], 71), 0)
    segment_ids = draw_segment_ids(jax.random.fold_in(key_of[12], 71), 0)
    first_weight = noise(key_of[3], (CH, 10), 10 ** -0.5, 2.0, ((0, 16),))
    first_bias = noise(key_of[4], (CH,), 0.5, 3.0, ((0, 16),))
    first_gain = jnp.clip(0.5 + 1.0 * jax.random.uniform(key_of[5], (CH,), jnp.float32) ** block_scale(key_of[5], (CH,), ((0, 16),), -0.2, 0.2), 0.5, 1.5).astype(jnp.bfloat16)
    first_shift = noise(key_of[6], (CH,), 0.5, 3.0, ((0, 16),))
    second_weight = noise(key_of[7], (CH, 3 * CH), (3 * CH) ** -0.5, 0.15625, ((0, 16),))
    second_bias = noise(key_of[8], (CH,), 0.5, 3.0, ((0, 16),))
    second_gain = jnp.clip(0.5 + 1.0 * jax.random.uniform(key_of[9], (CH,), jnp.float32) ** block_scale(key_of[9], (CH,), ((0, 16),), -0.2, 0.2), 0.5, 1.5).astype(jnp.bfloat16)
    second_shift = noise(key_of[10], (CH,), 0.5, 3.0, ((0, 16),))
    cotangent = bell_draw_with(key_of[11], (N_DP, N_FSDP * POS1, CH), ((N_DP * N_FSDP * POS1) ** -0.5), 0.01171875, ((0, 8), (1, 16)), (1, 2, 16, 2.0))
    return {"waveforms": waveforms, "packing_list": packing_list, "segment_ids": segment_ids, "first_weight": first_weight, "first_bias": first_bias, "first_gain": first_gain, "first_shift": first_shift, "second_weight": second_weight, "second_bias": second_bias, "second_gain": second_gain, "second_shift": second_shift, "cotangent": cotangent}


epsilon = 1e-05

def norm_act(pre_act, scale_by, shift_by, keep_rows):
    average = lax.optimization_barrier(jnp.mean(pre_act, axis=-1, keepdims=True))
    centred = pre_act - average
    spread = lax.optimization_barrier(jnp.mean(centred * centred, axis=-1, keepdims=True))
    scaled = centred * lax.rsqrt(spread + epsilon) * scale_by + shift_by
    return jax.nn.gelu(scaled, approximate=False) * keep_rows[:, None]

def frame_masks(segment, per_frame):
    following = jnp.concatenate([segment[1:], jnp.full((1,), -1, jnp.int32)])
    ending = following != segment
    places = jnp.arange(per_frame, dtype=jnp.int32)
    keeping = (segment >= 0)[:, None] & jnp.logical_not(ending[:, None] & (places == per_frame - 1)[None, :])
    return keeping.reshape(-1).astype(jnp.float32)

def read_offsets(source, length):
    ordinal = jnp.arange(source.shape[0], dtype=jnp.int32)
    earlier = ordinal[None, :] < ordinal[:, None]
    same_source = source[None, :] == source[:, None]
    return lax.optimization_barrier(jnp.sum(jnp.where(earlier & same_source, length[None, :], 0), axis=1)).astype(jnp.int32)

def owner_pass(packed, segment, params, cotangent_block):
    kernel_one, bias_one, gain_one, shift_one, kernel_two, bias_two, gain_two, shift_two = params
    channels = kernel_two.shape[0]
    keep_first = frame_masks(segment, 64)
    keep_second = frame_masks(segment, 32)
    blocks = packed.reshape(-1, 5)
    following = jnp.concatenate([blocks[1:], jnp.zeros((1, 5), blocks.dtype)])
    patches = jnp.concatenate([blocks, following], axis=1)
    pre_first = lax.dot_general(patches, kernel_one, (((1,), (1,)), ((), ())), preferred_element_type=jnp.float32)
    pre_first = pre_first + bias_one.astype(jnp.float32)
    post_first, back_first = jax.vjp(partial(norm_act, keep_rows=keep_first), pre_first, gain_one.astype(jnp.float32), shift_one.astype(jnp.float32))
    hidden = post_first.astype(jnp.bfloat16)
    paired = hidden.reshape(-1, 2 * channels)
    next_row = jnp.concatenate([paired[1:, :channels], jnp.zeros((1, channels), jnp.bfloat16)])
    columns = jnp.concatenate([paired, next_row], axis=1)
    pre_second = lax.dot_general(columns, kernel_two, (((1,), (1,)), ((), ())), preferred_element_type=jnp.float32)
    pre_second = pre_second + bias_two.astype(jnp.float32)
    post_second, back_second = jax.vjp(partial(norm_act, keep_rows=keep_second), pre_second, gain_two.astype(jnp.float32), shift_two.astype(jnp.float32))
    features = post_second.astype(jnp.bfloat16)
    grad_pre_two, grad_gain_two, grad_shift_two = back_second(cotangent_block.astype(jnp.float32))
    grad_bias_two = lax.optimization_barrier(jnp.sum(grad_pre_two, axis=0))
    grad_second = grad_pre_two.astype(jnp.bfloat16)
    grad_kernel_two = lax.dot_general(grad_second, columns, (((0,), (0,)), ((), ())), preferred_element_type=jnp.float32)
    grad_columns = jnp.dot(grad_second, kernel_two, preferred_element_type=jnp.float32)
    shifted = jnp.concatenate([jnp.zeros((1, channels), jnp.float32), grad_columns[:-1, 2 * channels:]])
    grad_hidden = (grad_columns[:, :2 * channels] + jnp.concatenate([shifted, jnp.zeros_like(shifted)], axis=1)).reshape(-1, channels)
    grad_pre_one, grad_gain_one, grad_shift_one = back_first(grad_hidden)
    grad_bias_one = lax.optimization_barrier(jnp.sum(grad_pre_one, axis=0))
    grad_first = grad_pre_one.astype(jnp.bfloat16)
    grad_kernel_one = lax.dot_general(grad_first, patches, (((0,), (0,)), ((), ())), preferred_element_type=jnp.float32)
    return (features, (grad_kernel_one, grad_bias_one, grad_gain_one, grad_shift_one, grad_kernel_two, grad_bias_two, grad_gain_two, grad_shift_two))

def reference(waveforms, packing_list, segment_ids, first_weight, first_bias, first_gain, first_shift, second_weight, second_bias, second_gain, second_shift, cotangent):
    params = (first_weight, first_bias, first_gain, first_shift, second_weight, second_bias, second_gain, second_shift)
    position = jnp.arange(PACK_FR, dtype=jnp.int32)[:, None]

    def one_owner(totals, owner_index):
        row_owner = (owner_index // N_FSDP).astype(jnp.int32)
        column = (owner_index % N_FSDP).astype(jnp.int32)
        entries = lax.dynamic_slice_in_dim(packing_list, column * LIST, LIST, 1)
        source, owner_of, place_at, length = (entries[0], entries[1], entries[2], entries[3])
        read_at = read_offsets(source, length)
        readers = lax.dynamic_slice_in_dim(waveforms, column * PACK_FR, PACK_FR, 1).reshape(N_DP * PACK_FR, 320)
        covered = (owner_of[None, :] == row_owner) & (position >= place_at[None, :]) & (position < (place_at + length)[None, :])
        pick_rows = lax.optimization_barrier(jnp.sum(jnp.where(covered, (source * PACK_FR + read_at)[None, :] + position - place_at[None, :], 0), axis=1))
        packed = jnp.where(jnp.any(covered, axis=1)[:, None], readers[pick_rows], 0).astype(jnp.bfloat16)
        segment = lax.dynamic_slice(segment_ids, (row_owner, column * PACK_FR), (1, PACK_FR))[0]
        cotangent_block = lax.dynamic_slice(cotangent, (row_owner, column * POS1, jnp.int32(0)), (1, POS1, CH))[0]
        features, grads = owner_pass(packed, segment, params, cotangent_block)
        totals = tuple((total + grad for total, grad in zip(totals, grads)))
        return (totals, features)
    initial = (jnp.zeros((CH, 10), jnp.float32), jnp.zeros((CH,), jnp.float32), jnp.zeros((CH,), jnp.float32), jnp.zeros((CH,), jnp.float32), jnp.zeros((CH, 3 * CH), jnp.float32), jnp.zeros((CH,), jnp.float32), jnp.zeros((CH,), jnp.float32), jnp.zeros((CH,), jnp.float32))
    totals, stacked = lax.scan(one_owner, initial, jnp.arange(N_DP * N_FSDP, dtype=jnp.int32))
    features = stacked.reshape(N_DP, N_FSDP * POS1, CH)
    return (features, totals[0], totals[1], totals[2], totals[3], totals[4], totals[5], totals[6], totals[7])
```

```python
import jax
import jax.numpy as jnp
import numpy as np
from jax import lax
from jax.experimental import pallas as pl
from jax.experimental.pallas import tpu as pltpu
from jax.sharding import PartitionSpec as P

MESH = pl.DeviceIdType.MESH
F32, BF16, I32 = jnp.float32, jnp.bfloat16, jnp.int32
EXACT = lax.Precision.HIGHEST
CH, FRAMES, ROWS, TILE, STEPS = 512, 128, 4096, 256, 16
DP, FS = 8, 16
SHARD, SLOT, TAPS = 32, 16, 10
EPS = 1e-05
HALF = 0.7071067811865476
EXP_BY = -1.4426950408889634
EXP_PLUS = -0.32574806470870245


def mm(a, b, dims, precision=None):
    return lax.dot_general(
        a, b, (dims, ((), ())), precision=precision, preferred_element_type=F32
    )


def iota(shape, axis):
    return lax.broadcasted_iota(I32, shape, axis)


def patch_tables():
    lane = np.arange(384)
    at = np.arange(TILE + 16) % 32
    mask = (lane[None, :] // TAPS == at[:, None]) & (lane < 320)[None, :]
    mask |= (lane == 320)[None, :]
    mask |= (lane == 321)[None, :] & (at != 31)[:, None]
    mask |= (lane == 322)[None, :] & (at == 31)[:, None]
    pick = np.zeros((384, 384), np.float32)
    for group in (0, 16, 32):
        for sample in range(320):
            tap = sample % TAPS
            pick[sample, group + tap] = 1
            if tap >= 5:
                pick[sample, 128 + group + tap - 5] = 1
            else:
                pick[sample, 256 + group + tap + 5] = 1
    for lane_out in (48, 49):
        pick[320, lane_out] = 1
        pick[321, 128 + lane_out] = 1
        pick[322, 128 + lane_out] = 1
    return jnp.asarray(mask, BF16), jnp.asarray(pick, BF16)


def greet(dp, fs):
    barrier = pltpu.get_barrier_semaphore()
    for k in range(1, DP):
        pl.semaphore_signal(barrier, inc=1, device_id=(lax.rem(dp + k, DP), fs), device_id_type=MESH)
    for k in range(1, FS):
        pl.semaphore_signal(barrier, inc=1, device_id=(dp, lax.rem(fs + k, FS)), device_id_type=MESH)
    pl.semaphore_wait(barrier, DP + FS - 2)


def send(src, dst, send_sem, recv_sem, device):
    return pltpu.make_async_remote_copy(
        src_ref=src, dst_ref=dst, send_sem=send_sem, recv_sem=recv_sem,
        device_id=device, device_id_type=MESH,
    )


def centred_weights(small):
    centred = small - jnp.mean(small, axis=1, keepdims=True)
    return jnp.where(iota((16, CH), 0) <= TAPS, centred, 0.0)


def split(value):
    high = value.astype(BF16).astype(F32)
    return high, value - high


def first_kernel(
    list_ref, seg_ref, wave_ref, weight_ref, vec_ref, second_ref, mask_ref, pick_ref,
    he_ref, ho_ref, de_ref, do_ref, le_ref, lo_ref, small_ref, second_out,
    slots, heard, small_own, smalls, second_all, frames, rhs, quad,
    a2a_s, a2a_r, sm_s, sm_r, w_s, w_r, fw_s, fw_r, out_sem,
):
    step = pl.program_id(0)
    dp, fs = lax.axis_index("dp"), lax.axis_index("fsdp")
    core = lax.rem(dp, 2)
    sibling = dp + 1 - 2 * core
    half = pl.ds(pl.multiple_of(core * 768, 128), 768)

    def a2a_copy(k):
        target = lax.rem(dp + k, DP)
        return send(
            slots.at[pl.ds(pl.multiple_of(target * SLOT, SLOT), SLOT)],
            heard.at[pl.ds(pl.multiple_of(dp * SLOT, SLOT), SLOT)],
            a2a_s.at[k], a2a_r.at[k], (target, fs),
        )

    def small_copy(k):
        return send(small_own, smalls.at[fs], sm_s.at[k], sm_r.at[k], (dp, lax.rem(fs + k, FS)))

    def second_copy(k):
        rows = pl.ds(pl.multiple_of(fs * SHARD, SHARD), SHARD)
        return send(
            second_ref.at[:, half], second_all.at[rows, half],
            w_s.at[k], w_r.at[k], (dp, lax.rem(fs + k, FS)),
        )

    def forward_copy(k):
        rows = pl.ds(pl.multiple_of(lax.rem(fs + FS - k, FS) * SHARD, SHARD), SHARD)
        piece = second_all.at[rows, half]
        return send(piece, piece, fw_s.at[k], fw_r.at[k], (sibling, fs))

    @pl.when(step == 0)
    def _():
        table = list_ref[...].astype(F32)
        eye = iota((128, 128), 0) == iota((128, 128), 1)

        def row(i):
            return jnp.broadcast_to(table[i : i + 1], (128, 128))

        def col(value):
            return jnp.sum(jnp.where(eye, value, 0.0), axis=1, keepdims=True)

        source, owner, place, length = row(0), row(1), row(2), row(3)
        source_c, owner_c, length_c = col(source), col(owner), col(length)
        earlier = (iota((128, 128), 0) < iota((128, 128), 1)) & (source_c == source)
        read_at = jnp.sum(jnp.where(earlier, length_c, 0.0), axis=0, keepdims=True)
        slot_at = jnp.sum(
            jnp.where(earlier & (owner_c == owner), length_c, 0.0), axis=0, keepdims=True
        )
        read_at = jnp.broadcast_to(read_at, (128, 128))
        slot_at = jnp.broadcast_to(slot_at, (128, 128))
        row_at = iota((128, 128), 0)
        lane_f = iota((128, 128), 1).astype(F32)
        group = (row_at // SLOT).astype(F32)
        inner = (row_at % SLOT).astype(F32)
        me = dp.astype(F32)
        entry = (
            (owner == group) & (source == me)
            & (slot_at <= inner) & (inner < slot_at + length)
        )
        frame = jnp.sum(jnp.where(entry, read_at + inner - slot_at + 1.0, 0.0), axis=1, keepdims=True)
        pack = jnp.where(lane_f + 1.0 == frame, 1.0, 0.0).astype(BF16)
        slots[...] = mm(pack, wave_ref[0], ((1,), (0,))).astype(BF16)

        place_lanes = jnp.where(
            iota((SHARD, 128), 1) == iota((SHARD, 128), 0) + lax.rem(fs, 4) * SHARD, 1.0, 0.0
        ).astype(BF16)
        quad[0:TAPS, 0:128] = mm(weight_ref[...], place_lanes, ((0,), (0,)))
        quad[TAPS:16, 0:128] = mm(vec_ref[...], place_lanes, ((1,), (0,)))
        small_own[...] = quad[0:16, 0:128].astype(BF16)

        greet(dp, fs)
        for k in range(1, DP):
            a2a_copy(k).start()
        for k in range(1, FS):
            small_copy(k).start()
        for k in range(1, FS):
            second_copy(k).start()

        mine = pl.ds(pl.multiple_of(dp * SLOT, SLOT), SLOT)
        heard[mine] = slots[mine]
        smalls[pl.ds(fs, 1)] = small_own[...][None]
        second_all[pl.ds(pl.multiple_of(fs * SHARD, SHARD), SHARD)] = second_ref[...]

        position = row_at.astype(F32)
        entry = (owner == me) & (position >= place) & (position < place + length)
        origin = jnp.sum(
            jnp.where(entry, source * SLOT + slot_at + position - place + 1.0, 0.0),
            axis=1, keepdims=True,
        )
        unpack = jnp.where(lane_f + 1.0 == origin, 1.0, 0.0).astype(BF16)
        seg = jnp.broadcast_to(seg_ref[...].astype(F32), (128, 128))
        following = jnp.where(iota((128, 128), 1) == 127, -1.0, pltpu.roll(seg, 127, 1))
        inside = jnp.where(seg >= 0, 1.0, 0.0)
        inside_c = col(inside)
        kept_c = col(jnp.where(following != seg, 0.0, inside))
        lane = iota((128, 128), 1)
        flags = jnp.where(
            (lane == 64) | (lane == 65), inside_c, jnp.where(lane == 66, kept_c, 0.0)
        )

        for k in range(1, FS):
            small_copy(k).wait_recv()
        parts = []
        for g in range(4):
            total = smalls[4 * g].astype(F32)
            for q in range(1, 4):
                total = total + smalls[4 * g + q].astype(F32)
            parts.append(total)
        small = jnp.concatenate(parts, axis=1)
        small_ref[...] = small
        centred = centred_weights(small)
        high, low = split(centred * small[11:12] * HALF)
        shift_high, shift_low = split(small[12:13] * HALF)
        r16 = iota((16, CH), 0)
        shifts = jnp.where(r16 == 0, shift_high, jnp.where(r16 == 1, shift_low, 0.0))
        rhs[...] = jnp.concatenate(
            [high, low, high, shifts, jnp.zeros((64, CH), F32)], axis=0
        ).astype(BF16)
        wide = jnp.concatenate([centred, jnp.zeros((112, CH), F32)], axis=0)
        gram = mm(centred, wide, ((1,), (1,)), EXACT) * (1.0 / CH)
        gram_a, rest = split(gram)
        gram_b, gram_c = split(rest)
        quad[:, 0:128] = jnp.concatenate(
            [gram_a, gram_b, gram_c, jnp.zeros((80, 128), F32)], axis=0
        )
        quad[:, 128:256] = jnp.where(row_at == 48, 1.0, 0.0)

        for k in range(1, DP):
            a2a_copy(k).wait_recv()
        packed = mm(unpack, heard[...], ((1,), (0,)))
        frames[0:128, 256:384] = flags
        frames[0:128, 0:320] = packed
        frames[128:144, :] = jnp.zeros((16, 384), F32)

    few = frames[pl.ds(pl.multiple_of(step * 8, 8), 16)].astype(BF16)
    spread = iota((TILE + 16, 16), 0)
    start = iota((TILE + 16, 16), 1) * 32
    repeat = jnp.where((spread >= start) & (spread < start + 32), 1.0, 0.0).astype(BF16)
    wide = mm(repeat, few, ((1,), (0,))).astype(BF16) * mask_ref[...]
    taken = mm(wide, pick_ref[...], ((1,), (0,)))
    even = taken[:TILE, 0:128]
    odd = taken[:TILE, 128:256] + pltpu.roll(taken[:, 256:384], TILE + 15, 0)[:TILE]
    lane1 = iota((1, 128), 1)
    bias_lane = jnp.where((lane1 == 10) | (lane1 == 26) | (lane1 == 42), 1.0, 0.0)
    patch = jnp.concatenate([even, odd], axis=0) + bias_lane
    form = mm(patch.astype(BF16), quad[...].astype(BF16), ((1,), (0,)))
    var = jnp.sum(form[:, 0:128] * patch, axis=1, keepdims=True)
    scale = lax.rsqrt(jnp.maximum(var, 0.0) + EPS) * form[:, 128:256]
    scaled = patch * scale
    high, low = split(scaled)
    lane_t = iota((2 * TILE, 128), 1)
    left = jnp.where(lane_t < 32, high, jnp.where(lane_t < 48, low, patch)).astype(BF16)
    for part, (h_ref, d_ref, l_ref) in enumerate(((he_ref, de_ref, le_ref), (ho_ref, do_ref, lo_ref))):
        piece = left[part * TILE : (part + 1) * TILE]
        l_ref[...] = piece
        u = mm(piece, rhs[...], ((1,), (0,)))
        phi = HALF * lax.erf(u) + HALF
        h_ref[...] = (u * phi).astype(BF16)
        bell = jnp.exp2(u * u * EXP_BY + EXP_PLUS)
        d_ref[...] = (phi + u * bell).astype(BF16)

    @pl.when(step > 0)
    def _():
        second_copy(step).wait_recv()
        forward_copy(step).start()

    @pl.when(step == STEPS - 1)
    def _():
        for k in range(1, FS):
            forward_copy(k).wait_recv()
        out = pltpu.make_async_copy(second_all, second_out, out_sem)
        out.start()
        for k in range(1, DP):
            a2a_copy(k).wait_send()
        for k in range(1, FS):
            small_copy(k).wait_send()
            second_copy(k).wait_send()
            forward_copy(k).wait_send()
        out.wait()


def second_kernel(
    he_ref, ho_ref, halo_ref, lo_ref, cot_ref, weight_ref, small_ref,
    feat_ref, g_ref, gs_ref, sums_ref, carry,
):
    step = pl.program_id(0)

    @pl.when(step == 0)
    def _():
        sums_ref[...] = jnp.zeros_like(sums_ref)
        carry[...] = jnp.zeros_like(carry)

    bias = small_ref[13:14]
    gain = small_ref[14:15]
    shift = small_ref[15:16]
    keep = lo_ref[...].astype(F32)[:, 48:49]
    even = he_ref[...]
    pre = mm(even, weight_ref[:, 0:CH], ((1,), (1,))) + mm(ho_ref[...], weight_ref[:, CH : 2 * CH], ((1,), (1,)))
    halo = halo_ref[...]
    halo = jnp.where(step == STEPS - 1, jnp.zeros_like(halo), halo)
    third = mm(jnp.concatenate([even, halo], axis=0), weight_ref[:, 2 * CH :], ((1,), (1,)))
    pre = pre + pltpu.roll(third, TILE + 15, 0)[:TILE] + bias
    centred = pre - jnp.mean(pre, axis=1, keepdims=True)
    var = jnp.mean(centred * centred, axis=1, keepdims=True)
    scale = lax.rsqrt(var + EPS)
    norm = centred * scale
    u = norm * (gain * HALF) + shift * HALF
    phi = HALF * lax.erf(u) + HALF
    feat_ref[0] = (u * phi * keep).astype(BF16)
    bell = jnp.exp2(u * u * EXP_BY + EXP_PLUS)
    slope = phi + u * bell
    dnorm = cot_ref[0].astype(F32) * (keep * HALF) * slope * gain
    prod = dnorm * norm
    mean_a = jnp.mean(dnorm, axis=1, keepdims=True)
    mean_b = jnp.mean(prod, axis=1, keepdims=True)
    dpre = (dnorm - mean_a - norm * mean_b) * scale
    sums_ref[0:8] += jnp.sum(dpre.reshape(TILE // 8, 8, CH), axis=0)
    sums_ref[8:16] += jnp.sum(prod.reshape(TILE // 8, 8, CH), axis=0)
    sums_ref[16:24] += jnp.sum(dnorm.reshape(TILE // 8, 8, CH), axis=0)
    g_ref[...] = dpre.astype(BF16)
    rolled = pltpu.roll(dpre, 1, 0)
    rolled = jnp.where(iota((TILE, CH), 0) == 0, carry[0:1], rolled)
    gs_ref[...] = rolled.astype(BF16)
    carry[0:1] = dpre[TILE - 1 : TILE]


def third_kernel(
    he_in, ho_in, g_in, gs_in, de_in, do_in, le_in, lo_in, weight_ref, small_ref, sums_ref,
    second_grad, first_grad, vec_b, vec_g, vec_s, vec_b2, vec_g2, vec_s2,
    he, ho, g1, gs, de, do, le, lo, total, half_bf, pair_in, pair_sum, y_in, y_sum, f_in, f_sum,
    gathered, wz, t_acc, r_acc, small_own, small_in, small_sum, small_dp,
    load, p_s, p_r, y_s, y_r, f_s, f_r, d_s, d_r, s_s, s_r, e_s, e_r,
):
    dp, fs = lax.axis_index("dp"), lax.axis_index("fsdp")
    core = lax.rem(dp, 2)
    yy = dp // 2
    sibling = dp + 1 - 2 * core
    quarter = pl.ds(pl.multiple_of(yy * 384, 128), 384)
    parts = ROWS // 4

    def chunk(k):
        return pl.ds(k * parts, parts)

    def chunk_loads(k):
        return [
            pltpu.make_async_copy(src.at[chunk(k)], dst.at[chunk(k)], load.at[i, k])
            for i, (src, dst) in enumerate(((g_in, g1), (gs_in, gs), (he_in, he), (ho_in, ho)))
        ]

    late = [
        pltpu.make_async_copy(src, dst, load.at[4 + i, 0])
        for i, (src, dst) in enumerate(((de_in, de), (do_in, do), (le_in, le), (lo_in, lo)))
    ]
    for k in range(4):
        for copy in chunk_loads(k):
            copy.start()
    for copy in late:
        copy.start()
    greet(dp, fs)

    def pair_copy(m):
        four = pl.ds(m * 4, 4)
        return send(half_bf.at[four, 1 - core], pair_in.at[four], p_s.at[m], p_r.at[m], (sibling, fs))

    def y_copy(k):
        target = lax.rem(yy + k, 4)
        return send(
            pair_sum.at[:, :, pl.ds(pl.multiple_of(target * 384, 128), 384)], y_in.at[k],
            y_s.at[k], y_r.at[k], (target * 2 + core, fs),
        )

    def f_copy(k):
        target = lax.rem(fs + k, FS)
        return send(y_sum.at[target], f_in.at[k], f_s.at[k], f_r.at[k], (dp, target))

    def d_copy(k):
        rows = pl.ds(pl.multiple_of(core * 16, 16), 16)
        return send(f_sum, gathered.at[rows, quarter], d_s.at[k], d_r.at[k], (lax.rem(dp + k, DP), fs))

    def s_copy(k):
        target = lax.rem(fs + k, FS)
        return send(small_own.at[target // 4], small_in.at[k], s_s.at[k], s_r.at[k], (dp, target))

    def e_copy(k):
        return send(small_sum, small_dp.at[k], e_s.at[k], e_r.at[k], (lax.rem(dp + k, DP), fs))

    small = small_ref[...]
    centred = centred_weights(small)
    gain = small[11:12]
    high, low = split(centred * gain)
    r16 = iota((16, CH), 0)
    wz[...] = jnp.concatenate(
        [high, low, high, jnp.where(r16 == 0, gain, 0.0), jnp.zeros((64, CH), F32)], axis=0
    ).astype(BF16)
    t_acc[...] = jnp.zeros_like(t_acc)
    r_acc[...] = jnp.zeros_like(r_acc)

    for k in range(4):
        for copy in chunk_loads(k):
            copy.wait()

        def block(m, _, k=k):
            cols = pl.ds(pl.multiple_of(m * 128, 128), 128)
            rows = chunk(k)
            g_part, gs_part = g1[rows, cols], gs[rows, cols]
            for c, (left, right) in enumerate(((g_part, he), (g_part, ho), (gs_part, he))):
                lanes = pl.ds(c * CH, CH)
                value = mm(left, right[rows], ((0,), (0,)))
                if k > 0:
                    value = value + total[cols, lanes]
                if k < 3:
                    total[cols, lanes] = value
                else:
                    half_bf[pl.ds(m * 4, 4), :, :, lanes] = value.astype(BF16).reshape(4, 2, 16, CH)
            if k == 3:
                pair_copy(m).start()
            return 0

        lax.fori_loop(0, 4, block, 0)
    for copy in late:
        copy.wait()

    def tile(i, _):
        rows = pl.ds(pl.multiple_of(i * TILE, TILE), TILE)
        g_tile = g1[rows]
        d_even = mm(g_tile, weight_ref[:, 0:CH], ((1,), (0,))) + mm(gs[rows], weight_ref[:, 2 * CH :], ((1,), (0,)))
        d_odd = mm(g_tile, weight_ref[:, CH : 2 * CH], ((1,), (0,)))
        lane = iota((TILE, 128), 1)
        for d_hidden, slope, lhs in ((d_even, de, le), (d_odd, do, lo)):
            ds = (d_hidden * slope[rows].astype(F32)).astype(BF16)
            left = lhs[rows]
            left_f = left.astype(F32)
            z = mm(ds, wz[...], ((1,), (1,)))
            inner = jnp.where(lane < 48, z * left_f, 0.0)
            corr = jnp.sum(inner, axis=1, keepdims=True)
            y = jnp.where(lane < 48, corr * left_f, z).astype(BF16)
            t_acc[...] += mm(left, ds, ((0,), (0,)))
            r_acc[...] += mm(y, left, ((0,), (0,)))

        @pl.when(i == 2)
        def _():
            for m in range(4):
                pair_copy(m).wait_recv()
                four = pl.ds(m * 4, 4)
                pair_sum[four] = (
                    half_bf[four, core].astype(F32) + pair_in[four].astype(F32)
                ).astype(BF16)
            for k in range(1, 4):
                y_copy(k).start()

        @pl.when(i == 9)
        def _():
            value = pair_sum[:, :, quarter].astype(F32)
            for k in range(1, 4):
                y_copy(k).wait_recv()
                value = value + y_in[k].astype(F32)
            y_sum[...] = value
            for k in range(1, FS):
                f_copy(k).start()

        @pl.when(i == 13)
        def _():
            value = y_sum[fs]
            for k in range(1, FS):
                f_copy(k).wait_recv()
                value = value + f_in[k]
            f_sum[...] = value
            for k in range(1, DP):
                d_copy(k).start()

        return 0

    lax.fori_loop(0, STEPS, tile, 0)

    t_core = t_acc[0:16] + t_acc[32:48]
    r_rows = jnp.concatenate(
        [r_acc[0:16] + r_acc[32:48], jnp.where(iota((8, 128), 0) == 0, r_acc[48:56], 0.0)], axis=0
    )
    r_rows = r_rows + pltpu.roll(r_rows, 96, 1)
    right = jnp.concatenate([centred, jnp.where(iota((8, CH), 0) == 0, 1.0, 0.0)], axis=0)
    corr = mm(r_rows, right, ((0,), (0,)), EXACT)[0:16] * (1.0 / CH)
    grad = (gain * t_core - corr) * HALF
    gain_grad = jnp.sum(centred * t_core, axis=0, keepdims=True) * HALF
    shift_grad = t_acc[48:49] * HALF
    sums = sums_ref[...]
    inv = 1.0 / small[14:15]
    grad = jnp.where(r16 == 11, gain_grad, grad)
    grad = jnp.where(r16 == 12, shift_grad, grad)
    grad = jnp.where(r16 == 13, jnp.sum(sums[0:8], axis=0, keepdims=True), grad)
    grad = jnp.where(r16 == 14, jnp.sum(sums[8:16], axis=0, keepdims=True) * inv, grad)
    grad = jnp.where(r16 == 15, jnp.sum(sums[16:24], axis=0, keepdims=True) * inv, grad)
    for q in range(4):
        small_own[q] = grad[:, q * 128 : (q + 1) * 128]
    for k in range(1, FS):
        s_copy(k).start()

    rows16 = pl.ds(pl.multiple_of(core * 16, 16), 16)
    gathered[rows16, quarter] = f_sum[...]
    for k in range(1, DP):
        d_copy(k).wait_recv()
    second_grad[...] = gathered[...]

    value = small_own[fs // 4]
    for k in range(1, FS):
        s_copy(k).wait_recv()
        value = value + small_in[k]
    small_sum[...] = value
    for k in range(1, DP):
        e_copy(k).start()
    for m in range(4):
        pair_copy(m).wait_send()
    for k in range(1, 4):
        y_copy(k).wait_send()
    for k in range(1, FS):
        f_copy(k).wait_send()
        s_copy(k).wait_send()
    for k in range(1, DP):
        d_copy(k).wait_send()
        e_copy(k).wait_recv()
        value = value + small_dp[k]
    for k in range(1, DP):
        e_copy(k).wait_send()
    own = pltpu.roll(value, lax.rem(128 - lax.rem(fs, 4) * SHARD, 128), 1)
    flipped = jnp.concatenate([own, jnp.zeros((112, 128), F32)], axis=0).T
    first_grad[...] = flipped[0:SHARD, 0:TAPS]
    for ref, at in zip((vec_b, vec_g, vec_s, vec_b2, vec_g2, vec_s2), range(10, 16)):
        ref[...] = own[at : at + 1, 0:SHARD]


def whole(shape):
    return pl.BlockSpec(shape, lambda i: (0,) * len(shape))


def local(
    waveforms, packing_list, segment_ids, first_weight, first_bias, first_gain, first_shift,
    second_weight, second_bias, second_gain, second_shift, cotangent,
):
    vecs = jnp.stack([first_bias, first_gain, first_shift, second_bias, second_gain, second_shift])
    mask, pick = patch_tables()
    shape = jax.ShapeDtypeStruct
    dma = pltpu.SemaphoreType.DMA
    rows = lambda width: pl.BlockSpec((TILE, width), lambda i: (i, 0))
    wide = shape((ROWS, CH), BF16)
    narrow = shape((ROWS, 128), BF16)
    anywhere = pl.BlockSpec(memory_space=pl.ANY)
    he, ho, de, do, le, lo, small, second = pl.pallas_call(
        first_kernel,
        grid=(STEPS,),
        out_shape=[wide, wide, wide, wide, narrow, narrow, shape((16, CH), F32), shape((CH, 3 * CH), BF16)],
        in_specs=[
            whole((4, 128)), whole((1, 128)), whole((1, FRAMES, 320)), whole((SHARD, TAPS)), whole((6, SHARD)),
            whole((SHARD, 3 * CH)), whole((TILE + 16, 384)), whole((384, 384)),
        ],
        out_specs=[rows(CH), rows(CH), rows(CH), rows(CH), rows(128), rows(128), whole((16, CH)), anywhere],
        scratch_shapes=[
            pltpu.VMEM((128, 320), BF16), pltpu.VMEM((128, 320), BF16),
            pltpu.VMEM((16, 128), BF16), pltpu.VMEM((FS, 16, 128), BF16),
            pltpu.VMEM((CH, 3 * CH), BF16), pltpu.VMEM((144, 384), F32),
            pltpu.VMEM((128, CH), BF16), pltpu.VMEM((128, 256), F32),
            dma((DP,)), dma((DP,)), dma((FS,)), dma((FS,)), dma((FS,)), dma((FS,)), dma((FS,)), dma((FS,)), dma,
        ],
        compiler_params=pltpu.CompilerParams(
            collective_id=0, has_side_effects=True, vmem_limit_bytes=48 << 20
        ),
    )(packing_list, segment_ids, waveforms, first_weight, vecs, second_weight, mask, pick)

    features, g1, gs, sums = pl.pallas_call(
        second_kernel,
        grid=(STEPS,),
        out_shape=[shape((1, ROWS, CH), BF16), wide, wide, shape((24, CH), F32)],
        in_specs=[
            rows(CH), rows(CH),
            pl.BlockSpec((16, CH), lambda i: (jnp.minimum((i + 1) * (TILE // 16), ROWS // 16 - 1), 0)),
            rows(128), pl.BlockSpec((1, TILE, CH), lambda i: (0, i, 0)),
            whole((CH, 3 * CH)), whole((16, CH)),
        ],
        out_specs=[pl.BlockSpec((1, TILE, CH), lambda i: (0, i, 0)), rows(CH), rows(CH), whole((24, CH))],
        scratch_shapes=[pltpu.VMEM((8, CH), F32)],
        compiler_params=pltpu.CompilerParams(vmem_limit_bytes=48 << 20),
    )(he, ho, he, lo, cotangent, second, small)

    vmem = pl.BlockSpec(memory_space=pltpu.VMEM)
    one = shape((1, SHARD), F32)
    second_grad, first_grad, b1, n1, s1, b2, n2, s2 = pl.pallas_call(
        third_kernel,
        out_shape=[shape((SHARD, 3 * CH), F32), shape((SHARD, TAPS), F32)] + [one] * 6,
        in_specs=[anywhere] * 8 + [vmem] * 3,
        out_specs=[vmem] * 8,
        scratch_shapes=[pltpu.VMEM((ROWS, CH), BF16)] * 6
        + [pltpu.VMEM((ROWS, 128), BF16)] * 2
        + [
            pltpu.VMEM((CH, 3 * CH), F32), pltpu.VMEM((FS, 2, 16, 3 * CH), BF16),
            pltpu.VMEM((FS, 16, 3 * CH), BF16), pltpu.VMEM((FS, 16, 3 * CH), BF16),
            pltpu.VMEM((4, FS, 16, 384), BF16), pltpu.VMEM((FS, 16, 384), F32),
            pltpu.VMEM((FS, 16, 384), F32), pltpu.VMEM((16, 384), F32),
            pltpu.VMEM((SHARD, 3 * CH), F32), pltpu.VMEM((128, CH), BF16),
            pltpu.VMEM((128, CH), F32), pltpu.VMEM((128, 128), F32),
            pltpu.VMEM((4, 16, 128), F32), pltpu.VMEM((FS, 16, 128), F32),
            pltpu.VMEM((16, 128), F32), pltpu.VMEM((DP, 16, 128), F32),
            dma((8, 4)), dma((4,)), dma((4,)), dma((4,)), dma((4,)), dma((FS,)), dma((FS,)),
            dma((DP,)), dma((DP,)), dma((FS,)), dma((FS,)), dma((DP,)), dma((DP,)),
        ],
        compiler_params=pltpu.CompilerParams(
            collective_id=1, has_side_effects=True, vmem_limit_bytes=56 << 20
        ),
    )(he, ho, g1, gs, de, do, le, lo, second, small, sums)
    flat = lambda value: value.reshape(SHARD)
    return (
        features, first_grad, flat(b1), flat(n1), flat(s1), second_grad, flat(b2), flat(n2), flat(s2),
    )


def solution(mesh):
    placed = (
        P("dp", "fsdp", None), P(None, "fsdp"), P("dp", "fsdp"), P("fsdp", None), P("fsdp"), P("fsdp"),
        P("fsdp"), P("fsdp", None), P("fsdp"), P("fsdp"), P("fsdp"), P("dp", "fsdp", None),
    )
    out = (
        P("dp", "fsdp", None), P("fsdp", None), P("fsdp"), P("fsdp"), P("fsdp"), P("fsdp", None),
        P("fsdp"), P("fsdp"), P("fsdp"),
    )
    return jax.shard_map(local, mesh=mesh, in_specs=placed, out_specs=out, check_vma=False)
```

```python
import jax
import jax.numpy as jnp
from jax import lax
from jax.experimental import pallas as pl
from jax.experimental.pallas import tpu as pltpu
from jax.sharding import PartitionSpec as P

MESH = pl.DeviceIdType.MESH
F32, BF16, I32 = jnp.float32, jnp.bfloat16, jnp.int32
EXACT = lax.Precision.HIGHEST
CH, FRAMES, ROWS, TILE, STEPS = 512, 128, 4096, 512, 8
PER_STEP = TILE // 32
PART = 256
VMEM_LIMIT = 60 << 20
FIRST, SECOND = STEPS, 2 * STEPS + 2
DP, FS = 8, 16
SHARD, SLOT, TAPS = 32, 16, 10
EPS = 1e-05
HALF = 0.7071067811865476
EXP_BY = -1.4426950408889634
EXP_PLUS = -0.32574806470870245


def mm(a, b, dims, precision=None):
    return lax.dot_general(
        a, b, (dims, ((), ())), precision=precision, preferred_element_type=F32
    )


def iota(shape, axis):
    return lax.broadcasted_iota(I32, shape, axis)


def patch_mask():
    shape = (TILE + 16, 384)
    lane = iota(shape, 1)
    at = iota(shape, 0) % 32
    first = at * TAPS
    on = (lane >= first) & (lane < first + TAPS) & (lane < 320)
    on |= lane == 320
    on |= (lane == 321) & (at != 31)
    on |= (lane == 322) & (at == 31)
    return jnp.where(on, 1.0, 0.0).astype(BF16)


def patch_pick():
    shape = (384, 384)
    sample = iota(shape, 0)
    out = iota(shape, 1)
    tap = sample - TAPS * ((sample * 6554) // 65536)
    block = out // 128
    lane = out % 128
    group = lane % 16
    within = (lane < 48) & (sample < 320)
    on = (block == 0) & (group < TAPS) & (tap == group)
    on |= (block == 1) & (group < 5) & (tap == group + 5)
    on |= (block == 2) & (group >= 5) & (group < TAPS) & (tap == group - 5)
    on &= within
    flag = (lane == 48) | (lane == 49)
    on |= flag & (block == 0) & (sample == 320)
    on |= flag & (block == 1) & ((sample == 321) | (sample == 322))
    return jnp.where(on, 1.0, 0.0).astype(BF16)


def along_x(fs, k):
    return fs // 4 * 4 + lax.rem(fs + k, 4)


def along_z(fs, k):
    return lax.rem(fs + 4 * k, FS)


def greet(dp, fs):
    barrier = pltpu.get_barrier_semaphore()
    for k in range(1, DP):
        pl.semaphore_signal(barrier, inc=1, device_id=(lax.rem(dp + k, DP), fs), device_id_type=MESH)
    for k in range(1, 4):
        pl.semaphore_signal(barrier, inc=1, device_id=(dp, along_x(fs, k)), device_id_type=MESH)
        pl.semaphore_signal(barrier, inc=1, device_id=(dp, along_z(fs, k)), device_id_type=MESH)


def all_here():
    pl.semaphore_wait(pltpu.get_barrier_semaphore(), DP - 1 + 6)


def send(src, dst, send_sem, recv_sem, device):
    return pltpu.make_async_remote_copy(
        src_ref=src, dst_ref=dst, send_sem=send_sem, recv_sem=recv_sem,
        device_id=device, device_id_type=MESH,
    )


def centred_weights(small):
    centred = small - jnp.mean(small, axis=1, keepdims=True)
    return jnp.where(iota((16, CH), 0) <= TAPS, centred, 0.0)


def split(value):
    high = value.astype(BF16).astype(F32)
    return high, value - high


def tile_rows(index):
    return pl.ds(pl.multiple_of(index * TILE, TILE), TILE)


def main_kernel(
    list_ref, seg_ref, wave_ref, weight_ref, vec_0, vec_1, vec_2, vec_3, vec_4, vec_5, second_ref, cot_ref,
    feat_ref, second_grad, vec_grad,
    slots, heard, part_own, smalls, part_row, part_rows, second_all, frames, rhs, quad, mask_ref, pick_ref, patches,
    small_ref, he, ho, de, do, le, lo, g1, gs,
    carry, total, sums_ref, pre_0, pre_1, g_0, g_1, gs_0, gs_1, grad_ref,
    even_0, even_1, odd_0, odd_1, pair_in, pair_sum, near_a, near_b, sum_a, sum_b,
    far_a, far_b, f_all, y_in, f_sum, gathered, wz, t_acc, r_acc,
    small_own, small_z, small_zsum, small_x, small_sum, small_dp,
    a2a_s, a2a_r, sm_s, sm_r, sz_0, sz_1, w_s, w_r, v_s, v_r, fw_s, fw_r,
    p_s, p_r, n_s, n_r, m_s, m_r, y_s, y_r, d_s, d_r, sz_s, sz_r, sx_s, sx_r, e_s, e_r,
):
    step = pl.program_id(0)
    dp, fs = lax.axis_index("dp"), lax.axis_index("fsdp")
    core = lax.rem(dp, 2)
    yy = dp // 2
    zz, xx = fs // 4, lax.rem(fs, 4)
    sibling = dp + 1 - 2 * core
    half = pl.ds(pl.multiple_of(core * 768, 128), 768)
    quarter = pl.ds(pl.multiple_of(yy * 384, 128), 384)
    pres, gs_pair = (pre_0, pre_1), ((g_0, gs_0), (g_1, gs_1))
    spreads = ((even_0, odd_0), (even_1, odd_1))

    def a2a_copy(k):
        target = lax.rem(dp + k, DP)
        return send(
            slots.at[pl.ds(pl.multiple_of(target * SLOT, SLOT), SLOT)],
            heard.at[pl.ds(pl.multiple_of(dp * SLOT, SLOT), SLOT)],
            a2a_s.at[k], a2a_r.at[k], (target, fs),
        )

    w_cols_a = pl.ds(pl.multiple_of(core * 768, 128), 384)
    w_cols_b = pl.ds(pl.multiple_of(core * 768 + 384, 128), 384)

    def part_x(k):
        return send(part_own, smalls.at[k], sm_s.at[k], sm_r.at[k], (dp, along_x(fs, k)))

    def part_z(k):
        return send(part_row, part_rows.at[zz], sz_0.at[k], sz_1.at[k], (dp, along_z(fs, k)))

    def near_weights(k):
        return (
            send(second_ref.at[:, w_cols_a], second_all.at[zz, xx, :, w_cols_a], w_s.at[0, k], w_r.at[0, k], (dp, along_x(fs, k))),
            send(second_ref.at[:, w_cols_b], second_all.at[zz, xx, :, w_cols_b], w_s.at[1, k], w_r.at[1, k], (dp, along_z(fs, k))),
        )

    def far_weights(k):
        piece_a = second_all.at[zz, :, :, w_cols_a]
        piece_b = second_all.at[:, xx, :, w_cols_b]
        return (
            send(piece_a, piece_a, v_s.at[0, k], v_r.at[0, k], (dp, along_z(fs, k))),
            send(piece_b, piece_b, v_s.at[1, k], v_r.at[1, k], (dp, along_x(fs, k))),
        )

    def forward_copy():
        piece = second_all.at[:, :, :, half]
        return send(piece, piece, fw_s, fw_r, (sibling, fs))

    @pl.when(step == 0)
    def _():
        greet(dp, fs)
        sums_ref[...] = jnp.zeros_like(sums_ref)
        carry[...] = jnp.zeros_like(carry)
        total[...] = jnp.zeros_like(total)
        he[ROWS:] = jnp.zeros((16, CH), BF16)
        t_acc[...] = jnp.zeros_like(t_acc)
        r_acc[...] = jnp.zeros_like(r_acc)
        table = list_ref[...].astype(F32)
        eye = iota((128, 128), 0) == iota((128, 128), 1)

        def row(i):
            return jnp.broadcast_to(table[i : i + 1], (128, 128))

        def col(value):
            return jnp.sum(jnp.where(eye, value, 0.0), axis=1, keepdims=True)

        source, owner, place, length = row(0), row(1), row(2), row(3)
        source_c, owner_c, length_c = col(source), col(owner), col(length)
        earlier = (iota((128, 128), 0) < iota((128, 128), 1)) & (source_c == source)
        read_at = jnp.sum(jnp.where(earlier, length_c, 0.0), axis=0, keepdims=True)
        slot_at = jnp.sum(
            jnp.where(earlier & (owner_c == owner), length_c, 0.0), axis=0, keepdims=True
        )
        read_at = jnp.broadcast_to(read_at, (128, 128))
        slot_at = jnp.broadcast_to(slot_at, (128, 128))
        row_at = iota((128, 128), 0)
        lane_f = iota((128, 128), 1).astype(F32)
        group = (row_at // SLOT).astype(F32)
        inner = (row_at % SLOT).astype(F32)
        me = dp.astype(F32)
        entry = (
            (owner == group) & (source == me)
            & (slot_at <= inner) & (inner < slot_at + length)
        )
        frame = jnp.sum(jnp.where(entry, read_at + inner - slot_at + 1.0, 0.0), axis=1, keepdims=True)
        pack = jnp.where(lane_f + 1.0 == frame, 1.0, 0.0).astype(BF16)
        slots[...] = mm(pack, wave_ref[...], ((1,), (1,))).astype(BF16)

        place_lanes = jnp.where(
            iota((SHARD, 128), 1) == iota((SHARD, 128), 0) + lax.rem(fs, 4) * SHARD, 1.0, 0.0
        ).astype(BF16)
        quad[0:TAPS, 0:128] = mm(weight_ref[...], place_lanes, ((1,), (0,)))
        frames[0:8, 0:128] = jnp.zeros((8, 128), F32)
        for at, ref in enumerate((vec_0, vec_1, vec_2, vec_3, vec_4, vec_5)):
            frames[at : at + 1, 0:SHARD] = ref[...].astype(F32)
        vecs = frames[0:8, 0:SHARD].astype(BF16)
        quad[TAPS:16, 0:128] = mm(vecs, place_lanes, ((1,), (0,)))[0:6]
        part_own[...] = quad[0:16, 0:128].astype(BF16)

        all_here()
        for k in range(1, 4):
            part_x(k).start()
        for k in range(1, DP):
            a2a_copy(k).start()
        for k in range(1, 4):
            for copy in near_weights(k):
                copy.start()
        mask_ref[...] = patch_mask()
        whole_row = part_own[...].astype(F32)
        for k in range(1, 4):
            part_x(k).wait_recv()
            whole_row = whole_row + smalls[k].astype(F32)
        part_row[...] = whole_row.astype(BF16)
        for k in range(1, 4):
            part_z(k).start()
        pick_ref[...] = patch_pick()
        mine = pl.ds(pl.multiple_of(dp * SLOT, SLOT), SLOT)
        heard[mine] = slots[mine]
        second_all[zz, xx, :, half] = second_ref[:, half]

        position = row_at.astype(F32)
        entry = (owner == me) & (position >= place) & (position < place + length)
        origin = jnp.sum(
            jnp.where(entry, source * SLOT + slot_at + position - place + 1.0, 0.0),
            axis=1, keepdims=True,
        )
        unpack = jnp.where(lane_f + 1.0 == origin, 1.0, 0.0).astype(BF16)
        seg = jnp.broadcast_to(seg_ref[...].astype(F32), (128, 128))
        following = jnp.where(iota((128, 128), 1) == 127, -1.0, pltpu.roll(seg, 127, 1))
        inside = jnp.where(seg >= 0, 1.0, 0.0)
        inside_c = col(inside)
        kept_c = col(jnp.where(following != seg, 0.0, inside))
        lane = iota((128, 128), 1)
        flags = jnp.where(
            (lane == 64) | (lane == 65), inside_c, jnp.where(lane == 66, kept_c, 0.0)
        )

        for k in range(1, DP):
            a2a_copy(k).wait_recv()
        packed = mm(unpack, heard[...], ((1,), (0,)))
        frames[0:128, 256:384] = flags
        frames[0:128, 0:320] = packed
        frames[128:144, :] = jnp.zeros((16, 384), F32)
        def cut(turn, _):
            few = frames[pl.ds(pl.multiple_of(turn * PER_STEP, PER_STEP), 32)].astype(BF16)
            spread = iota((TILE + 16, 32), 0)
            start = iota((TILE + 16, 32), 1) * 32
            repeat = jnp.where((spread >= start) & (spread < start + 32), 1.0, 0.0).astype(BF16)
            wide = mm(repeat, few, ((1,), (0,))).astype(BF16) * mask_ref[...]
            taken = mm(wide, pick_ref[...], ((1,), (0,)))
            even = taken[:TILE, 0:128]
            odd = taken[:TILE, 128:256] + pltpu.roll(taken[:, 256:384], TILE + 15, 0)[:TILE]
            lane1 = iota((1, 128), 1)
            bias_lane = jnp.where((lane1 == 10) | (lane1 == 26) | (lane1 == 42), 1.0, 0.0)
            patches[turn] = (jnp.concatenate([even, odd], axis=0) + bias_lane).astype(BF16)
            return 0

        lax.fori_loop(0, STEPS, cut, 0)

        part_rows[pl.ds(zz, 1)] = part_row[...][None]
        for k in range(1, 4):
            part_z(k).wait_recv()
        small = jnp.concatenate([part_rows[g].astype(F32) for g in range(4)], axis=1)
        small_ref[...] = small
        centred = centred_weights(small)
        high, low = split(centred * small[11:12] * HALF)
        shift_high, shift_low = split(small[12:13] * HALF)
        r16 = iota((16, CH), 0)
        shifts = jnp.where(r16 == 0, shift_high, jnp.where(r16 == 1, shift_low, 0.0))
        rhs[...] = jnp.concatenate(
            [high, low, high, shifts, jnp.zeros((64, CH), F32)], axis=0
        ).astype(BF16)
        wide = jnp.concatenate([centred, jnp.zeros((112, CH), F32)], axis=0)
        gram = mm(centred, wide, ((1,), (1,)), EXACT) * (1.0 / CH)
        gram_a, rest = split(gram)
        gram_b, gram_c = split(rest)
        quad[:, 0:128] = jnp.concatenate(
            [gram_a, gram_b, gram_c, jnp.zeros((80, 128), F32)], axis=0
        )
        quad[:, 128:256] = jnp.where(row_at == 48, 1.0, 0.0)

    @pl.when(step < STEPS)
    def _():
        patch_bf = patches[step]
        patch = patch_bf.astype(F32)
        form = mm(patch_bf, quad[...].astype(BF16), ((1,), (0,)))
        var = jnp.sum(form[:, 0:128] * patch, axis=1, keepdims=True)
        scale = lax.rsqrt(jnp.maximum(var, 0.0) + EPS) * form[:, 128:256]
        scaled = patch * scale
        high, low = split(scaled)
        lane_t = iota((2 * TILE, 128), 1)
        left = jnp.where(lane_t < 32, high, jnp.where(lane_t < 48, low, patch)).astype(BF16)
        rows = tile_rows(step)
        for part, (h_ref, d_ref, l_ref) in enumerate(((he, de, le), (ho, do, lo))):
            piece = left[part * TILE : (part + 1) * TILE]
            l_ref[rows] = piece
            u = mm(piece, rhs[...], ((1,), (0,)))
            phi = HALF * lax.erf(u) + HALF
            h_ref[rows] = (u * phi).astype(BF16)
            bell = jnp.exp2(u * u * EXP_BY + EXP_PLUS)
            d_ref[rows] = (phi + u * bell).astype(BF16)

    @pl.when(step == 1)
    def _():
        for k in range(1, 4):
            for copy in near_weights(k):
                copy.wait_recv()
        for k in range(1, 4):
            for copy in far_weights(k):
                copy.start()

    @pl.when(step == STEPS - 3)
    def _():
        for k in range(1, 4):
            for copy in far_weights(k):
                copy.wait_recv()
        forward_copy().start()

    @pl.when(step == STEPS - 1)
    def _():
        forward_copy().wait_recv()
        for k in range(1, DP):
            a2a_copy(k).wait_send()
        for k in range(1, 4):
            part_x(k).wait_send()
            part_z(k).wait_send()
            for copy in near_weights(k) + far_weights(k):
                copy.wait_send()
        forward_copy().wait_send()

    def pair_copy(m):
        return send(grad_ref.at[m, :, 1 - core], pair_in.at[m], p_s.at[m], p_r.at[m], (sibling, fs))

    cols_a, cols_b = pl.ds(0, 768), pl.ds(768, 768)

    def near_copies(k):
        z_to, x_to = lax.rem(zz + k, 4), lax.rem(xx + k, 4)
        return (
            send(pair_sum.at[z_to, :, :, cols_a], near_a.at[k], n_s.at[0, k], n_r.at[0, k], (dp, along_z(fs, k))),
            send(pair_sum.at[:, x_to, :, cols_b], near_b.at[k], n_s.at[1, k], n_r.at[1, k], (dp, along_x(fs, k))),
        )

    def far_copies(k):
        z_to, x_to = lax.rem(zz + k, 4), lax.rem(xx + k, 4)
        return (
            send(sum_a.at[x_to], far_a.at[k], m_s.at[0, k], m_r.at[0, k], (dp, along_x(fs, k))),
            send(sum_b.at[z_to], far_b.at[k], m_s.at[1, k], m_r.at[1, k], (dp, along_z(fs, k))),
        )

    def y_copy(k):
        target = lax.rem(yy + k, 4)
        return send(
            f_all.at[:, pl.ds(pl.multiple_of(target * 384, 128), 384)], y_in.at[k],
            y_s.at[k], y_r.at[k], (target * 2 + core, fs),
        )

    def d_copy(k):
        rows = pl.ds(pl.multiple_of(core * 16, 16), 16)
        return send(f_sum, gathered.at[rows, quarter], d_s.at[k], d_r.at[k], (lax.rem(dp + k, DP), fs))

    def sz_copy(k):
        return send(small_own.at[lax.rem(zz + k, 4)], small_z.at[k], sz_s.at[k], sz_r.at[k], (dp, along_z(fs, k)))

    def sx_copy(k):
        return send(small_zsum, small_x.at[k], sx_s.at[k], sx_r.at[k], (dp, along_x(fs, k)))

    def e_copy(k):
        return send(small_sum, small_dp.at[k], e_s.at[k], e_r.at[k], (lax.rem(dp + k, DP), fs))

    def taps(c):
        return second_all[:, :, :, c * CH : (c + 1) * CH].reshape(CH, CH)

    def convolve(slot):
        rows = tile_rows(step - FIRST)
        more = pl.ds(pl.multiple_of((step - FIRST) * TILE, TILE), TILE + 16)
        pre = mm(he[rows], taps(0), ((1,), (1,))) + mm(ho[rows], taps(1), ((1,), (1,)))
        third = mm(he[more], taps(2), ((1,), (1,)))
        pres[slot][...] = pre + pltpu.roll(third, TILE + 15, 0)[:TILE]

    def activate(slot):
        bias, gain, shift = small_ref[13:14], small_ref[14:15], small_ref[15:16]
        gain_u, shift_u = gain * HALF, shift * HALF
        last = carry[0:1]
        totals = [jnp.zeros((8, CH), F32)] * 3
        for part in range(TILE // PART):
            rows = pl.ds(part * PART, PART)
            far = pl.ds(pl.multiple_of((step - FIRST - 1) * TILE + part * PART, PART), PART)
            keep = lo[far].astype(F32)[:, 48:49]
            pre = pres[slot][rows] + bias
            centred = pre - jnp.mean(pre, axis=1, keepdims=True)
            var = jnp.mean(centred * centred, axis=1, keepdims=True)
            scale = lax.rsqrt(var + EPS)
            norm = centred * scale
            u = norm * gain_u + shift_u
            phi = HALF * lax.erf(u) + HALF
            feat_ref[0, rows] = (u * phi * keep).astype(BF16)
            bell = jnp.exp2(u * u * EXP_BY + EXP_PLUS)
            slope = phi + u * bell
            dnorm = cot_ref[0, rows].astype(F32) * (keep * HALF) * slope * gain
            prod = dnorm * norm
            mean_a = jnp.mean(dnorm, axis=1, keepdims=True)
            mean_b = jnp.mean(prod, axis=1, keepdims=True)
            dpre = (dnorm - mean_a - norm * mean_b) * scale
            for at, value in enumerate((dpre, prod, dnorm)):
                totals[at] = totals[at] + jnp.sum(value.reshape(PART // 8, 8, CH), axis=0)
            g1[far] = dpre.astype(BF16)
            gs_pair[slot][0][rows] = dpre.astype(BF16)
            rolled = pltpu.roll(dpre, 1, 0)
            rolled = jnp.where(iota((PART, CH), 0) == 0, last, rolled).astype(BF16)
            gs[far] = rolled
            gs_pair[slot][1][rows] = rolled
            last = dpre[PART - 1 : PART]
        carry[0:1] = last
        for at in range(3):
            sums_ref[at * 8 : at * 8 + 8] += totals[at]

    def weigh(slot):
        g_part, gs_part = gs_pair[slot]
        rows = tile_rows(step - FIRST - 2)
        for c, (left, right) in enumerate(((g_part, he), (g_part, ho), (gs_part, he))):
            total[:, c * CH : (c + 1) * CH] += mm(left[...], right[rows], ((0,), (0,)))

    at = step - FIRST

    @pl.when(at == 0)
    def _():
        convolve(0)

    @pl.when(at == 1)
    def _():
        convolve(1)
        activate(0)

    for slot in range(2):

        @pl.when((at >= 2) & (at < STEPS) & (at % 2 == slot))
        def _(slot=slot):
            convolve(slot)
            weigh(slot)
            activate(1 - slot)

    @pl.when(at == STEPS)
    def _():
        weigh(0)
        activate(1)

    @pl.when(at == STEPS + 1)
    def _():
        weigh(1)
        grad_ref[...] = total[...].astype(BF16).reshape(4, 4, 2, 16, 3 * CH)
        for m in range(4):
            pair_copy(m).start()

    def spread(slot):
        rows = tile_rows(step - SECOND)
        g_tile = g1[rows]
        even = mm(g_tile, taps(0), ((1,), (0,)))
        spreads[slot][0][...] = even + mm(gs[rows], taps(2), ((1,), (0,)))
        spreads[slot][1][...] = mm(g_tile, taps(1), ((1,), (0,)))

    def gather_terms(slot):
        lane = iota((TILE, 128), 1)
        rows = tile_rows(step - SECOND - 1)
        for d_hidden, slope, lhs in zip(spreads[slot], (de, do), (le, lo)):
            ds = (d_hidden[...] * slope[rows].astype(F32)).astype(BF16)
            left = lhs[rows]
            left_f = left.astype(F32)
            z = mm(ds, wz[...], ((1,), (1,)))
            inner = jnp.where(lane < 48, z * left_f, 0.0)
            corr = jnp.sum(inner, axis=1, keepdims=True)
            y = jnp.where(lane < 48, corr * left_f, z).astype(BF16)
            t_acc[...] += mm(left, ds, ((0,), (0,)))
            r_acc[...] += mm(y, left, ((0,), (0,)))

    then = step - SECOND

    @pl.when(then == 0)
    def _():
        small = small_ref[...]
        gain = small[11:12]
        high, low = split(centred_weights(small) * gain)
        wz[...] = jnp.concatenate(
            [high, low, high, jnp.where(iota((16, CH), 0) == 0, gain, 0.0), jnp.zeros((64, CH), F32)], axis=0
        ).astype(BF16)
        spread(0)

    for slot in range(2):

        @pl.when((then >= 1) & (then < STEPS) & (then % 2 == slot))
        def _(slot=slot):
            spread(slot)
            gather_terms(1 - slot)

    @pl.when(then == 1)
    def _():
        for m in range(4):
            pair_copy(m).wait_recv()
            pair_sum[m] = (grad_ref[m, :, core].astype(F32) + pair_in[m].astype(F32)).astype(BF16)
        for k in range(1, 4):
            for copy in near_copies(k):
                copy.start()

    @pl.when(then == 5)
    def _():
        value_a = pair_sum[zz, :, :, cols_a].astype(F32)
        value_b = pair_sum[:, xx, :, cols_b].astype(F32)
        for k in range(1, 4):
            for copy in near_copies(k):
                copy.wait_recv()
            value_a = value_a + near_a[k].astype(F32)
            value_b = value_b + near_b[k].astype(F32)
        sum_a[...] = value_a.astype(BF16)
        sum_b[...] = value_b.astype(BF16)
        for k in range(1, 4):
            for copy in far_copies(k):
                copy.start()

    @pl.when(then == 6)
    def _():
        value_a = sum_a[xx].astype(F32)
        value_b = sum_b[zz].astype(F32)
        for k in range(1, 4):
            for copy in far_copies(k):
                copy.wait_recv()
            value_a = value_a + far_a[k].astype(F32)
            value_b = value_b + far_b[k].astype(F32)
        f_all[:, cols_a] = value_a
        f_all[:, cols_b] = value_b
        for k in range(1, 4):
            y_copy(k).start()

    @pl.when(then == 7)
    def _():
        value = f_all[:, quarter]
        for k in range(1, 4):
            y_copy(k).wait_recv()
            value = value + y_in[k]
        f_sum[...] = value
        for k in range(1, DP):
            d_copy(k).start()

    @pl.when(then == STEPS)
    def _():
        gather_terms(1)
        small = small_ref[...]
        centred = centred_weights(small)
        gain = small[11:12]
        r16 = iota((16, CH), 0)
        t_core = t_acc[0:16] + t_acc[32:48]
        r_rows = jnp.concatenate(
            [r_acc[0:16] + r_acc[32:48], jnp.where(iota((8, 128), 0) == 0, r_acc[48:56], 0.0)], axis=0
        )
        r_rows = r_rows + pltpu.roll(r_rows, 96, 1)
        right = jnp.concatenate([centred, jnp.where(iota((8, CH), 0) == 0, 1.0, 0.0)], axis=0)
        corr = mm(r_rows, right, ((0,), (0,)), EXACT)[0:16] * (1.0 / CH)
        grad = (gain * t_core - corr) * HALF
        gain_grad = jnp.sum(centred * t_core, axis=0, keepdims=True) * HALF
        shift_grad = t_acc[48:49] * HALF
        sums = sums_ref[...]
        inv = 1.0 / small[14:15]
        grad = jnp.where(r16 == 11, gain_grad, grad)
        grad = jnp.where(r16 == 12, shift_grad, grad)
        grad = jnp.where(r16 == 13, jnp.sum(sums[0:8], axis=0, keepdims=True), grad)
        grad = jnp.where(r16 == 14, jnp.sum(sums[8:16], axis=0, keepdims=True) * inv, grad)
        grad = jnp.where(r16 == 15, jnp.sum(sums[16:24], axis=0, keepdims=True) * inv, grad)
        for q in range(4):
            small_own[q] = grad[:, q * 128 : (q + 1) * 128]
        for k in range(1, 4):
            sz_copy(k).start()

        rows16 = pl.ds(pl.multiple_of(core * 16, 16), 16)
        gathered[rows16, quarter] = f_sum[...]
        for k in range(1, DP):
            d_copy(k).wait_recv()
        second_grad[...] = gathered[...]
        value = small_own[zz]
        for k in range(1, 4):
            sz_copy(k).wait_recv()
            value = value + small_z[k]
        small_zsum[...] = value
        for k in range(1, 4):
            sx_copy(k).start()
        for m in range(4):
            pair_copy(m).wait_send()
        for k in range(1, 4):
            for copy in near_copies(k) + far_copies(k):
                copy.wait_send()
            y_copy(k).wait_send()
            sz_copy(k).wait_send()
        for k in range(1, 4):
            sx_copy(k).wait_recv()
            value = value + small_x[k]
        small_sum[...] = value
        for k in range(1, DP):
            e_copy(k).start()
        for k in range(1, DP):
            d_copy(k).wait_send()
        for k in range(1, 4):
            sx_copy(k).wait_send()
        for k in range(1, DP):
            e_copy(k).wait_recv()
            value = value + small_dp[k]
        for k in range(1, DP):
            e_copy(k).wait_send()
        vec_grad[...] = pltpu.roll(value, lax.rem(128 - lax.rem(fs, 4) * SHARD, 128), 1)


def last_kernel(feat_in, second_in, vec_in, feat_out, second_grad, first_grad, *rest):
    *vecs, stage, sems_in, sems_out = rest
    rows = [pl.ds(k * TILE, TILE) for k in range(STEPS)]
    loads = [pltpu.make_async_copy(feat_in.at[:, r], stage.at[:, r], sems_in.at[k]) for k, r in enumerate(rows)]
    stores = [pltpu.make_async_copy(stage.at[:, r], feat_out.at[:, r], sems_out.at[k]) for k, r in enumerate(rows)]
    for copy in loads:
        copy.start()
    for load, store in zip(loads, stores):
        load.wait()
        store.start()
    second_grad[...] = second_in[...]
    first_grad[...] = vec_in[0:TAPS, 0:SHARD]
    for at, ref in enumerate(vecs):
        ref[...] = vec_in[TAPS + at : TAPS + at + 1, 0:SHARD]
    for copy in stores:
        copy.wait()


def whole(shape):
    return pl.BlockSpec(shape, lambda i: (0,) * len(shape))


def local(
    waveforms, packing_list, segment_ids, first_weight, first_bias, first_gain, first_shift,
    second_weight, second_bias, second_gain, second_shift, cotangent,
):
    vecs = (first_bias, first_gain, first_shift, second_bias, second_gain, second_shift)
    vecs = [value.reshape(1, SHARD) for value in vecs]
    shape = jax.ShapeDtypeStruct
    dma = pltpu.SemaphoreType.DMA

    def block(i):
        return (0, jnp.clip(i - FIRST - 1, 0, STEPS - 1), 0)

    def vmem(kind, *dims):
        return pltpu.VMEM(dims, kind)

    features, second_grad, vec_grad = pl.pallas_call(
        main_kernel,
        grid=(SECOND + STEPS + 1,),
        out_shape=[shape((1, ROWS, CH), BF16), shape((SHARD, 3 * CH), F32), shape((16, 128), F32)],
        in_specs=[
            whole((4, 128)), whole((1, 128)), whole((320, FRAMES)), whole((TAPS, SHARD)),
            *([whole((1, SHARD))] * 6), whole((SHARD, 3 * CH)), pl.BlockSpec((1, TILE, CH), block),
        ],
        out_specs=[pl.BlockSpec((1, TILE, CH), block), whole((SHARD, 3 * CH)), whole((16, 128))],
        scratch_shapes=[
            vmem(BF16, 128, 320), vmem(BF16, 128, 320), vmem(BF16, 16, 128), vmem(BF16, 4, 16, 128),
            vmem(BF16, 16, 128), vmem(BF16, 4, 16, 128), vmem(BF16, 4, 4, SHARD, 3 * CH), vmem(F32, 144, 384),
            vmem(BF16, 128, CH), vmem(F32, 128, 256), vmem(BF16, TILE + 16, 384), vmem(BF16, 384, 384),
            vmem(BF16, STEPS, 2 * TILE, 128),
            vmem(F32, 16, CH), vmem(BF16, ROWS + 16, CH), vmem(BF16, ROWS, CH), vmem(BF16, ROWS, CH),
            vmem(BF16, ROWS, CH), vmem(BF16, ROWS, 128), vmem(BF16, ROWS, 128), vmem(BF16, ROWS, CH),
            vmem(BF16, ROWS, CH),
            vmem(F32, 8, CH), vmem(F32, CH, 3 * CH), vmem(F32, 24, CH), vmem(F32, TILE, CH), vmem(F32, TILE, CH),
            vmem(BF16, TILE, CH), vmem(BF16, TILE, CH), vmem(BF16, TILE, CH), vmem(BF16, TILE, CH),
            vmem(BF16, 4, 4, 2, 16, 3 * CH),
            vmem(F32, TILE, CH), vmem(F32, TILE, CH), vmem(F32, TILE, CH), vmem(F32, TILE, CH),
            vmem(BF16, 4, 4, 16, 3 * CH), vmem(BF16, 4, 4, 16, 3 * CH),
            vmem(BF16, 4, 4, 16, 768), vmem(BF16, 4, 4, 16, 768),
            vmem(BF16, 4, 16, 768), vmem(BF16, 4, 16, 768), vmem(BF16, 4, 16, 768), vmem(BF16, 4, 16, 768),
            vmem(F32, 16, 3 * CH), vmem(F32, 4, 16, 384), vmem(F32, 16, 384),
            vmem(F32, SHARD, 3 * CH), vmem(BF16, 128, CH), vmem(F32, 128, CH), vmem(F32, 128, 128),
            vmem(F32, 4, 16, 128), vmem(F32, 4, 16, 128), vmem(F32, 16, 128),
            vmem(F32, 4, 16, 128), vmem(F32, 16, 128), vmem(F32, DP, 16, 128),
            dma((DP,)), dma((DP,)), dma((4,)), dma((4,)), dma((4,)), dma((4,)),
            dma((2, 4)), dma((2, 4)), dma((2, 4)), dma((2, 4)), dma, dma,
            dma((4,)), dma((4,)), dma((2, 4)), dma((2, 4)), dma((2, 4)), dma((2, 4)),
            dma((4,)), dma((4,)), dma((DP,)), dma((DP,)),
            dma((4,)), dma((4,)), dma((4,)), dma((4,)), dma((DP,)), dma((DP,)),
        ],
        compiler_params=pltpu.CompilerParams(
            collective_id=0, has_side_effects=True, vmem_limit_bytes=VMEM_LIMIT
        ),
    )(packing_list, segment_ids, waveforms[0].T, first_weight.T, *vecs, second_weight, cotangent)

    one = shape((1, SHARD), F32)
    anywhere = pl.BlockSpec(memory_space=pl.ANY)
    local_vmem = pl.BlockSpec(memory_space=pltpu.VMEM)
    outs = pl.pallas_call(
        last_kernel,
        out_shape=[shape((1, ROWS, CH), BF16), shape((SHARD, 3 * CH), F32), shape((TAPS, SHARD), F32)] + [one] * 6,
        in_specs=[anywhere, local_vmem, local_vmem],
        out_specs=[anywhere] + [local_vmem] * 8,
        scratch_shapes=[pltpu.VMEM((1, ROWS, CH), BF16), dma((STEPS,)), dma((STEPS,))],
        compiler_params=pltpu.CompilerParams(vmem_limit_bytes=VMEM_LIMIT),
    )(features, second_grad, vec_grad)
    b1, n1, s1, b2, n2, s2 = [value.reshape(SHARD) for value in outs[3:]]
    return outs[0], outs[2].T, b1, n1, s1, outs[1], b2, n2, s2


def solution(mesh):
    placed = (
        P("dp", "fsdp", None), P(None, "fsdp"), P("dp", "fsdp"), P("fsdp", None), P("fsdp"), P("fsdp"),
        P("fsdp"), P("fsdp", None), P("fsdp"), P("fsdp"), P("fsdp"), P("dp", "fsdp", None),
    )
    out = (
        P("dp", "fsdp", None), P("fsdp", None), P("fsdp"), P("fsdp"), P("fsdp"), P("fsdp", None),
        P("fsdp"), P("fsdp"), P("fsdp"),
    )
    return jax.shard_map(local, mesh=mesh, in_specs=placed, out_specs=out, check_vma=False)
```

```python
import jax
import jax.numpy as jnp
from jax import lax
from jax.experimental import pallas as pl
from jax.experimental.pallas import tpu as pltpu
from jax.sharding import PartitionSpec as P

MESH = pl.DeviceIdType.MESH
F32, BF16, I32 = jnp.float32, jnp.bfloat16, jnp.int32
EXACT = lax.Precision.HIGHEST
CH, FRAMES, ROWS, TILE, STEPS = 512, 128, 4096, 512, 8
PER_STEP = TILE // 32
PART = 128
VMEM_LIMIT = 60 << 20
DP, FS = 8, 16
SHARD, SLOT, TAPS = 32, 16, 10
EPS = 1e-05
HALF = 0.7071067811865476
EXP_BY = -1.4426950408889634
EXP_PLUS = -0.32574806470870245


def mm(a, b, dims, precision=None):
    return lax.dot_general(
        a, b, (dims, ((), ())), precision=precision, preferred_element_type=F32
    )


def iota(shape, axis):
    return lax.broadcasted_iota(I32, shape, axis)


def patch_mask():
    shape = (TILE + 16, 384)
    lane = iota(shape, 1)
    at = iota(shape, 0) % 32
    first = at * TAPS
    on = (lane >= first) & (lane < first + TAPS) & (lane < 320)
    on |= lane == 320
    on |= (lane == 321) & (at != 31)
    on |= (lane == 322) & (at == 31)
    return jnp.where(on, 1.0, 0.0).astype(BF16)


def patch_pick():
    shape = (384, 384)
    sample = iota(shape, 0)
    out = iota(shape, 1)
    tap = sample - TAPS * ((sample * 6554) // 65536)
    block = out // 128
    lane = out % 128
    group = lane % 16
    within = (lane < 48) & (sample < 320)
    on = (block == 0) & (group < TAPS) & (tap == group)
    on |= (block == 1) & (group < 5) & (tap == group + 5)
    on |= (block == 2) & (group >= 5) & (group < TAPS) & (tap == group - 5)
    on &= within
    flag = (lane == 48) | (lane == 49)
    on |= flag & (block == 0) & (sample == 320)
    on |= flag & (block == 1) & ((sample == 321) | (sample == 322))
    return jnp.where(on, 1.0, 0.0).astype(BF16)


def along_x(fs, k):
    return fs // 4 * 4 + lax.rem(fs + k, 4)


def along_z(fs, k):
    return lax.rem(fs + 4 * k, FS)


def greet(dp, fs):
    barrier = pltpu.get_barrier_semaphore()
    for k in range(1, DP):
        pl.semaphore_signal(barrier, inc=1, device_id=(lax.rem(dp + k, DP), fs), device_id_type=MESH)
    for k in range(1, 4):
        pl.semaphore_signal(barrier, inc=1, device_id=(dp, along_x(fs, k)), device_id_type=MESH)
        pl.semaphore_signal(barrier, inc=1, device_id=(dp, along_z(fs, k)), device_id_type=MESH)


def all_here():
    pl.semaphore_wait(pltpu.get_barrier_semaphore(), DP - 1 + 6)


def send(src, dst, send_sem, recv_sem, device):
    return pltpu.make_async_remote_copy(
        src_ref=src, dst_ref=dst, send_sem=send_sem, recv_sem=recv_sem,
        device_id=device, device_id_type=MESH,
    )


def centred_weights(small):
    centred = small - jnp.mean(small, axis=1, keepdims=True)
    return jnp.where(iota((16, CH), 0) <= TAPS, centred, 0.0)


def split(value):
    high = value.astype(BF16).astype(F32)
    return high, value - high


def weave(*lists):
    queue = []
    for jobs in lists:
        queue += [((at + 0.5) / len(jobs), job) for at, job in enumerate(jobs)]
    for _, job in sorted(queue, key=lambda entry: entry[0]):
        job()


def tile_rows(index):
    return pl.ds(pl.multiple_of(index * TILE, TILE), TILE)


def main_kernel(
    list_ref, seg_ref, wave_ref, weight_ref, vec_0, vec_1, vec_2, vec_3, vec_4, vec_5, second_ref, cot_ref,
    feat_ref, second_grad, vec_grad,
    slots, heard, part_own, smalls, part_row, part_rows, second_all, frames, rhs, quad, mask_ref, pick_ref, patches,
    small_ref, he, ho, de, do, le, lo, g1, gs,
    carry, total, sums_ref, pre_0, pre_1, g_0, g_1, gs_0, gs_1, grad_ref,
    even_0, even_1, odd_0, odd_1, pair_in, pair_sum, near_a, near_b, sum_a, sum_b,
    far_a, far_b, f_all, y_in, f_sum, gathered, wz, t_acc, r_acc,
    small_own, small_z, small_zsum, small_x, small_sum, small_dp,
    a2a_s, a2a_r, sm_s, sm_r, sz_0, sz_1, w_s, w_r, v_s, v_r, fw_s, fw_r,
    p_s, p_r, n_s, n_r, m_s, m_r, y_s, y_r, d_s, d_r, sz_s, sz_r, sx_s, sx_r, e_s, e_r,
):
    step = pl.program_id(0)
    dp, fs = lax.axis_index("dp"), lax.axis_index("fsdp")
    core = lax.rem(dp, 2)
    yy = dp // 2
    zz, xx = fs // 4, lax.rem(fs, 4)
    sibling = dp + 1 - 2 * core
    half = pl.ds(pl.multiple_of(core * 768, 128), 768)
    quarter = pl.ds(pl.multiple_of(yy * 384, 128), 384)
    pres, gs_pair = (pre_0, pre_1), ((g_0, gs_0), (g_1, gs_1))
    spreads = ((even_0, odd_0), (even_1, odd_1))

    def a2a_copy(k):
        target = lax.rem(dp + k, DP)
        return send(
            slots.at[pl.ds(pl.multiple_of(target * SLOT, SLOT), SLOT)],
            heard.at[pl.ds(pl.multiple_of(dp * SLOT, SLOT), SLOT)],
            a2a_s.at[k], a2a_r.at[k], (target, fs),
        )

    w_cols_a = pl.ds(pl.multiple_of(core * 768, 128), 384)
    w_cols_b = pl.ds(pl.multiple_of(core * 768 + 384, 128), 384)

    def part_x(k):
        return send(part_own, smalls.at[k], sm_s.at[k], sm_r.at[k], (dp, along_x(fs, k)))

    def part_z(k):
        return send(part_row, part_rows.at[zz], sz_0.at[k], sz_1.at[k], (dp, along_z(fs, k)))

    def near_weights(k):
        return (
            send(second_ref.at[:, w_cols_a], second_all.at[zz, xx, :, w_cols_a], w_s.at[0, k], w_r.at[0, k], (dp, along_x(fs, k))),
            send(second_ref.at[:, w_cols_b], second_all.at[zz, xx, :, w_cols_b], w_s.at[1, k], w_r.at[1, k], (dp, along_z(fs, k))),
        )

    def far_weights(k):
        piece_a = second_all.at[zz, :, :, w_cols_a]
        piece_b = second_all.at[:, xx, :, w_cols_b]
        return (
            send(piece_a, piece_a, v_s.at[0, k], v_r.at[0, k], (dp, along_z(fs, k))),
            send(piece_b, piece_b, v_s.at[1, k], v_r.at[1, k], (dp, along_x(fs, k))),
        )

    def forward_copy():
        piece = second_all.at[:, :, :, half]
        return send(piece, piece, fw_s, fw_r, (sibling, fs))

    @pl.when(step == 0)
    def _():
        greet(dp, fs)
        sums_ref[...] = jnp.zeros_like(sums_ref)
        carry[...] = jnp.zeros_like(carry)
        total[...] = jnp.zeros_like(total)
        he[ROWS:] = jnp.zeros((16, CH), BF16)
        t_acc[...] = jnp.zeros_like(t_acc)
        r_acc[...] = jnp.zeros_like(r_acc)
        table = list_ref[...].astype(F32)
        eye = iota((128, 128), 0) == iota((128, 128), 1)

        def row(i):
            return jnp.broadcast_to(table[i : i + 1], (128, 128))

        def col(value):
            return jnp.sum(jnp.where(eye, value, 0.0), axis=1, keepdims=True)

        source, owner, place, length = row(0), row(1), row(2), row(3)
        source_c, owner_c, length_c = col(source), col(owner), col(length)
        earlier = (iota((128, 128), 0) < iota((128, 128), 1)) & (source_c == source)
        read_at = jnp.sum(jnp.where(earlier, length_c, 0.0), axis=0, keepdims=True)
        slot_at = jnp.sum(
            jnp.where(earlier & (owner_c == owner), length_c, 0.0), axis=0, keepdims=True
        )
        read_at = jnp.broadcast_to(read_at, (128, 128))
        slot_at = jnp.broadcast_to(slot_at, (128, 128))
        row_at = iota((128, 128), 0)
        lane_f = iota((128, 128), 1).astype(F32)
        group = (row_at // SLOT).astype(F32)
        inner = (row_at % SLOT).astype(F32)
        me = dp.astype(F32)
        entry = (
            (owner == group) & (source == me)
            & (slot_at <= inner) & (inner < slot_at + length)
        )
        frame = jnp.sum(jnp.where(entry, read_at + inner - slot_at + 1.0, 0.0), axis=1, keepdims=True)
        pack = jnp.where(lane_f + 1.0 == frame, 1.0, 0.0).astype(BF16)
        slots[...] = mm(pack, wave_ref[...], ((1,), (1,))).astype(BF16)

        place_lanes = jnp.where(
            iota((SHARD, 128), 1) == iota((SHARD, 128), 0) + lax.rem(fs, 4) * SHARD, 1.0, 0.0
        ).astype(BF16)
        quad[0:TAPS, 0:128] = mm(weight_ref[...], place_lanes, ((1,), (0,)))
        frames[0:8, 0:128] = jnp.zeros((8, 128), F32)
        for at, ref in enumerate((vec_0, vec_1, vec_2, vec_3, vec_4, vec_5)):
            frames[at : at + 1, 0:SHARD] = ref[...].astype(F32)
        vecs = frames[0:8, 0:SHARD].astype(BF16)
        quad[TAPS:16, 0:128] = mm(vecs, place_lanes, ((1,), (0,)))[0:6]
        part_own[...] = quad[0:16, 0:128].astype(BF16)

        all_here()
        for k in range(1, 4):
            part_x(k).start()
        for k in range(1, DP):
            a2a_copy(k).start()
        for k in range(1, 4):
            for copy in near_weights(k):
                copy.start()
        mask_ref[...] = patch_mask()
        whole_row = part_own[...].astype(F32)
        for k in range(1, 4):
            part_x(k).wait_recv()
            whole_row = whole_row + smalls[k].astype(F32)
        part_row[...] = whole_row.astype(BF16)
        for k in range(1, 4):
            part_z(k).start()
        pick_ref[...] = patch_pick()
        mine = pl.ds(pl.multiple_of(dp * SLOT, SLOT), SLOT)
        heard[mine] = slots[mine]
        second_all[zz, xx, :, half] = second_ref[:, half]

        position = row_at.astype(F32)
        entry = (owner == me) & (position >= place) & (position < place + length)
        origin = jnp.sum(
            jnp.where(entry, source * SLOT + slot_at + position - place + 1.0, 0.0),
            axis=1, keepdims=True,
        )
        unpack = jnp.where(lane_f + 1.0 == origin, 1.0, 0.0).astype(BF16)
        seg = jnp.broadcast_to(seg_ref[...].astype(F32), (128, 128))
        following = jnp.where(iota((128, 128), 1) == 127, -1.0, pltpu.roll(seg, 127, 1))
        inside = jnp.where(seg >= 0, 1.0, 0.0)
        inside_c = col(inside)
        kept_c = col(jnp.where(following != seg, 0.0, inside))
        lane = iota((128, 128), 1)
        flags = jnp.where(
            (lane == 64) | (lane == 65), inside_c, jnp.where(lane == 66, kept_c, 0.0)
        )

        for k in range(1, DP):
            a2a_copy(k).wait_recv()
        packed = mm(unpack, heard[...], ((1,), (0,)))
        frames[0:128, 256:384] = flags
        frames[0:128, 0:320] = packed
        frames[128:144, :] = jnp.zeros((16, 384), F32)
        def cut(turn, _):
            few = frames[pl.ds(pl.multiple_of(turn * PER_STEP, PER_STEP), 32)].astype(BF16)
            spread = iota((TILE + 16, 32), 0)
            start = iota((TILE + 16, 32), 1) * 32
            repeat = jnp.where((spread >= start) & (spread < start + 32), 1.0, 0.0).astype(BF16)
            wide = mm(repeat, few, ((1,), (0,))).astype(BF16) * mask_ref[...]
            taken = mm(wide, pick_ref[...], ((1,), (0,)))
            even = taken[:TILE, 0:128]
            odd = taken[:TILE, 128:256] + pltpu.roll(taken[:, 256:384], TILE + 15, 0)[:TILE]
            lane1 = iota((1, 128), 1)
            bias_lane = jnp.where((lane1 == 10) | (lane1 == 26) | (lane1 == 42), 1.0, 0.0)
            patches[turn] = (jnp.concatenate([even, odd], axis=0) + bias_lane).astype(BF16)
            return 0

        lax.fori_loop(0, STEPS, cut, 0)

        part_rows[pl.ds(zz, 1)] = part_row[...][None]
        for k in range(1, 4):
            part_z(k).wait_recv()
        small = jnp.concatenate([part_rows[g].astype(F32) for g in range(4)], axis=1)
        small_ref[...] = small
        centred = centred_weights(small)
        high, low = split(centred * small[11:12] * HALF)
        shift_high, shift_low = split(small[12:13] * HALF)
        r16 = iota((16, CH), 0)
        shifts = jnp.where(r16 == 0, shift_high, jnp.where(r16 == 1, shift_low, 0.0))
        rhs[...] = jnp.concatenate(
            [high, low, high, shifts, jnp.zeros((64, CH), F32)], axis=0
        ).astype(BF16)
        wide = jnp.concatenate([centred, jnp.zeros((112, CH), F32)], axis=0)
        gram = mm(centred, wide, ((1,), (1,)), EXACT) * (1.0 / CH)
        gram_a, rest = split(gram)
        gram_b, gram_c = split(rest)
        quad[:, 0:128] = jnp.concatenate(
            [gram_a, gram_b, gram_c, jnp.zeros((80, 128), F32)], axis=0
        )
        quad[:, 128:256] = jnp.where(row_at == 48, 1.0, 0.0)

    def first_block(turn, _):
        patch_bf = patches[turn]
        patch = patch_bf.astype(F32)
        form = mm(patch_bf, quad[...].astype(BF16), ((1,), (0,)))
        var = jnp.sum(form[:, 0:128] * patch, axis=1, keepdims=True)
        scale = lax.rsqrt(jnp.maximum(var, 0.0) + EPS) * form[:, 128:256]
        scaled = patch * scale
        high, low = split(scaled)
        lane_t = iota((2 * TILE, 128), 1)
        left = jnp.where(lane_t < 32, high, jnp.where(lane_t < 48, low, patch)).astype(BF16)
        rows = tile_rows(turn)
        for part, (h_ref, d_ref, l_ref) in enumerate(((he, de, le), (ho, do, lo))):
            piece = left[part * TILE : (part + 1) * TILE]
            l_ref[rows] = piece
            u = mm(piece, rhs[...], ((1,), (0,)))
            phi = HALF * lax.erf(u) + HALF
            h_ref[rows] = (u * phi).astype(BF16)
            bell = jnp.exp2(u * u * EXP_BY + EXP_PLUS)
            d_ref[rows] = (phi + u * bell).astype(BF16)
        return 0

    @pl.when(step == 0)
    def _():
        lax.fori_loop(0, 2, first_block, 0)
        for k in range(1, 4):
            for copy in near_weights(k):
                copy.wait_recv()
        for k in range(1, 4):
            for copy in far_weights(k):
                copy.start()
        lax.fori_loop(2, 6, first_block, 0)
        for k in range(1, 4):
            for copy in far_weights(k):
                copy.wait_recv()
        forward_copy().start()
        lax.fori_loop(6, STEPS, first_block, 0)
        for k in range(1, DP):
            a2a_copy(k).wait_send()
        for k in range(1, 4):
            part_x(k).wait_send()
            part_z(k).wait_send()
            for copy in near_weights(k) + far_weights(k):
                copy.wait_send()
        forward_copy().wait_recv()
        forward_copy().wait_send()

    def pair_copy(m):
        return send(grad_ref.at[m, :, 1 - core], pair_in.at[m], p_s.at[m], p_r.at[m], (sibling, fs))

    cols_a, cols_b = pl.ds(0, 768), pl.ds(768, 768)

    def near_copies(k):
        z_to, x_to = lax.rem(zz + k, 4), lax.rem(xx + k, 4)
        return (
            send(pair_sum.at[z_to, :, :, cols_a], near_a.at[k], n_s.at[0, k], n_r.at[0, k], (dp, along_z(fs, k))),
            send(pair_sum.at[:, x_to, :, cols_b], near_b.at[k], n_s.at[1, k], n_r.at[1, k], (dp, along_x(fs, k))),
        )

    def far_copies(k):
        z_to, x_to = lax.rem(zz + k, 4), lax.rem(xx + k, 4)
        return (
            send(sum_a.at[x_to], far_a.at[k], m_s.at[0, k], m_r.at[0, k], (dp, along_x(fs, k))),
            send(sum_b.at[z_to], far_b.at[k], m_s.at[1, k], m_r.at[1, k], (dp, along_z(fs, k))),
        )

    def y_copy(k):
        target = lax.rem(yy + k, 4)
        return send(
            f_all.at[:, pl.ds(pl.multiple_of(target * 384, 128), 384)], y_in.at[k],
            y_s.at[k], y_r.at[k], (target * 2 + core, fs),
        )

    def d_copy(k):
        rows = pl.ds(pl.multiple_of(core * 16, 16), 16)
        return send(f_sum, gathered.at[rows, quarter], d_s.at[k], d_r.at[k], (lax.rem(dp + k, DP), fs))

    def sz_copy(k):
        return send(small_own.at[lax.rem(zz + k, 4)], small_z.at[k], sz_s.at[k], sz_r.at[k], (dp, along_z(fs, k)))

    def sx_copy(k):
        return send(small_zsum, small_x.at[k], sx_s.at[k], sx_r.at[k], (dp, along_x(fs, k)))

    def e_copy(k):
        return send(small_sum, small_dp.at[k], e_s.at[k], e_r.at[k], (lax.rem(dp + k, DP), fs))

    def taps(c, n=None):
        if n is None:
            return second_all[:, :, :, c * CH : (c + 1) * CH].reshape(CH, CH)
        return second_all[2 * n : 2 * n + 2, :, :, c * CH : (c + 1) * CH].reshape(CH // 2, CH)

    def convolve(slot):
        rows = tile_rows(step)
        more = pl.ds(pl.multiple_of((step) * TILE, TILE), TILE + 16)
        kept = {}

        def third():
            kept[0] = pltpu.roll(mm(he[more], taps(2), ((1,), (1,))), TILE + 15, 0)[:TILE]

        def first():
            kept[1] = mm(he[rows], taps(0), ((1,), (1,)))

        def rest():
            pres[slot][...] = kept[1] + mm(ho[rows], taps(1), ((1,), (1,))) + kept[0]

        return [third, first, rest]

    def activate(slot):
        bias, gain, shift = small_ref[13:14], small_ref[14:15], small_ref[15:16]
        gain_u, shift_u = gain * HALF, shift * HALF
        state = {"last": carry[0:1]}

        def norms(part):
            rows = pl.ds(part * PART, PART)
            pre = pres[slot][rows] + bias
            centred = pre - jnp.mean(pre, axis=1, keepdims=True)
            var = jnp.mean(centred * centred, axis=1, keepdims=True)
            scale = lax.rsqrt(var + EPS)
            norm = centred * scale
            state[part] = (norm, scale)

        def slopes(part):
            rows = pl.ds(part * PART, PART)
            far = pl.ds(pl.multiple_of((step - 1) * TILE + part * PART, PART), PART)
            keep = lo[far].astype(F32)[:, 48:49]
            norm, scale = state[part]
            u = norm * gain_u + shift_u
            phi = HALF * lax.erf(u) + HALF
            feat_ref[0, rows] = (u * phi * keep).astype(BF16)
            bell = jnp.exp2(u * u * EXP_BY + EXP_PLUS)
            slope = phi + u * bell
            dnorm = cot_ref[0, rows].astype(F32) * (keep * HALF) * slope * gain
            prod = dnorm * norm
            mean_a = jnp.mean(dnorm, axis=1, keepdims=True)
            mean_b = jnp.mean(prod, axis=1, keepdims=True)
            state[part, 1] = (norm, scale, dnorm, prod, mean_a, mean_b)

        def finish(part):
            rows = pl.ds(part * PART, PART)
            far = pl.ds(pl.multiple_of((step - 1) * TILE + part * PART, PART), PART)
            norm, scale, dnorm, prod, mean_a, mean_b = state[part, 1]
            dpre = (dnorm - mean_a - norm * mean_b) * scale
            for at, value in enumerate((dpre, prod, dnorm)):
                sums_ref[at * 8 : at * 8 + 8] += jnp.sum(value.reshape(PART // 8, 8, CH), axis=0)
            here = dpre.astype(BF16)
            g1[far] = here
            gs_pair[slot][0][rows] = here
            rolled = pltpu.roll(dpre, 1, 0)
            rolled = jnp.where(iota((PART, CH), 0) == 0, state["last"], rolled).astype(BF16)
            gs[far] = rolled
            gs_pair[slot][1][rows] = rolled
            state["last"] = dpre[PART - 1 : PART]
            if part == TILE // PART - 1:
                carry[0:1] = state["last"]

        jobs = []
        count = TILE // PART
        for turn in range(count + 2):
            for lag, job in ((0, norms), (1, slopes), (2, finish)):
                if 0 <= turn - lag < count:
                    jobs.append(lambda job=job, part=turn - lag: job(part))
        return jobs

    def weigh(slot):
        g_part, gs_part = gs_pair[slot]
        rows = tile_rows(step - 2)

        def run(c, n):
            left, right = ((g_part, he), (g_part, ho), (gs_part, he))[c]
            cols = slice(n * 256, n * 256 + 256)
            total[:, c * CH + n * 256 : c * CH + n * 256 + 256] += mm(left[...], right[rows, cols], ((0,), (0,)))

        return [lambda c=c, n=n: run(c, n) for c in range(3) for n in range(2)]

    @pl.when(step == 0)
    def _():
        weave(convolve(0))

    @pl.when(step == 1)
    def _():
        weave(convolve(1), activate(0))

    for slot in range(2):

        @pl.when((step >= 2) & (step < STEPS) & (step % 2 == slot))
        def _(slot=slot):
            weave(convolve(slot) + weigh(slot), activate(1 - slot))

    @pl.when(step == STEPS)
    def _():
        weave(weigh(0), activate(1))

    @pl.when(step == STEPS + 1)
    def _():
        weave(weigh(1))
        grad_ref[...] = total[...].astype(BF16).reshape(4, 4, 2, 16, 3 * CH)
        for m in range(4):
            pair_copy(m).start()

    def spread(slot, turn):
        rows = tile_rows(turn)

        kept = {}

        def even(n):
            cols = slice(n * 256, n * 256 + 256)
            kept[n] = mm(g1[rows], taps(0)[:, cols], ((1,), (0,)))

        def more(n):
            cols = slice(n * 256, n * 256 + 256)
            spreads[slot][0][:, cols] = kept[n] + mm(gs[rows], taps(2)[:, cols], ((1,), (0,)))

        def odd(n):
            cols = slice(n * 256, n * 256 + 256)
            spreads[slot][1][:, cols] = mm(g1[rows], taps(1)[:, cols], ((1,), (0,)))

        order = ((even, 0), (more, 0), (even, 1), (more, 1), (odd, 0), (odd, 1))
        return [lambda job=job, n=n: job(n) for job, n in order]

    def gather_terms(slot, turn):
        size = TILE
        lane = iota((size, 128), 1)

        def run(parity, part):
            near = pl.ds(part * size, size)
            rows = pl.ds(pl.multiple_of(turn * TILE + part * size, size), size)
            slope, lhs = ((de, le), (do, lo))[parity]
            ds = (spreads[slot][parity][near] * slope[rows].astype(F32)).astype(BF16)
            left = lhs[rows]
            left_f = left.astype(F32)
            z = mm(ds, wz[...], ((1,), (1,)))
            inner = jnp.where(lane < 48, z * left_f, 0.0)
            corr = jnp.sum(inner, axis=1, keepdims=True)
            y = jnp.where(lane < 48, corr * left_f, z).astype(BF16)
            t_acc[...] += mm(left, ds, ((0,), (0,)))
            r_acc[...] += mm(y, left, ((0,), (0,)))

        return [lambda a=a, b=b: run(a, b) for a in range(2) for b in range(1)]

    @pl.when(step == STEPS + 1)
    def _():
        def both(slot, turn):
            weave(spread(slot, turn), gather_terms(1 - slot, turn - 1))

        def pair(turn, _):
            both(0, 2 * turn)
            both(1, 2 * turn + 1)
            return 0

        small = small_ref[...]
        gain = small[11:12]
        high, low = split(centred_weights(small) * gain)
        wz[...] = jnp.concatenate(
            [high, low, high, jnp.where(iota((16, CH), 0) == 0, gain, 0.0), jnp.zeros((64, CH), F32)], axis=0
        ).astype(BF16)
        weave(spread(0, 0))
        both(1, 1)
        for m in range(4):
            pair_copy(m).wait_recv()
            pair_sum[m] = (grad_ref[m, :, core].astype(F32) + pair_in[m].astype(F32)).astype(BF16)
        for k in range(1, 4):
            for copy in near_copies(k):
                copy.start()
        lax.fori_loop(1, 3, pair, 0)
        value_a = pair_sum[zz, :, :, cols_a].astype(F32)
        value_b = pair_sum[:, xx, :, cols_b].astype(F32)
        for k in range(1, 4):
            for copy in near_copies(k):
                copy.wait_recv()
            value_a = value_a + near_a[k].astype(F32)
            value_b = value_b + near_b[k].astype(F32)
        sum_a[...] = value_a.astype(BF16)
        sum_b[...] = value_b.astype(BF16)
        for k in range(1, 4):
            for copy in far_copies(k):
                copy.start()
        both(0, 6)
        value_a = sum_a[xx].astype(F32)
        value_b = sum_b[zz].astype(F32)
        for k in range(1, 4):
            for copy in far_copies(k):
                copy.wait_recv()
            value_a = value_a + far_a[k].astype(F32)
            value_b = value_b + far_b[k].astype(F32)
        f_all[:, cols_a] = value_a
        f_all[:, cols_b] = value_b
        for k in range(1, 4):
            y_copy(k).start()
        both(1, 7)
        value = f_all[:, quarter]
        for k in range(1, 4):
            y_copy(k).wait_recv()
            value = value + y_in[k]
        f_sum[...] = value
        for k in range(1, DP):
            d_copy(k).start()
        weave(gather_terms(1, STEPS - 1))
        small = small_ref[...]
        centred = centred_weights(small)
        gain = small[11:12]
        r16 = iota((16, CH), 0)
        t_core = t_acc[0:16] + t_acc[32:48]
        r_rows = jnp.concatenate(
            [r_acc[0:16] + r_acc[32:48], jnp.where(iota((8, 128), 0) == 0, r_acc[48:56], 0.0)], axis=0
        )
        r_rows = r_rows + pltpu.roll(r_rows, 96, 1)
        right = jnp.concatenate([centred, jnp.where(iota((8, CH), 0) == 0, 1.0, 0.0)], axis=0)
        corr = mm(r_rows, right, ((0,), (0,)), EXACT)[0:16] * (1.0 / CH)
        grad = (gain * t_core - corr) * HALF
        gain_grad = jnp.sum(centred * t_core, axis=0, keepdims=True) * HALF
        shift_grad = t_acc[48:49] * HALF
        sums = sums_ref[...]
        inv = 1.0 / small[14:15]
        grad = jnp.where(r16 == 11, gain_grad, grad)
        grad = jnp.where(r16 == 12, shift_grad, grad)
        grad = jnp.where(r16 == 13, jnp.sum(sums[0:8], axis=0, keepdims=True), grad)
        grad = jnp.where(r16 == 14, jnp.sum(sums[8:16], axis=0, keepdims=True) * inv, grad)
        grad = jnp.where(r16 == 15, jnp.sum(sums[16:24], axis=0, keepdims=True) * inv, grad)
        for q in range(4):
            small_own[q] = grad[:, q * 128 : (q + 1) * 128]
        for k in range(1, 4):
            sz_copy(k).start()

        rows16 = pl.ds(pl.multiple_of(core * 16, 16), 16)
        gathered[rows16, quarter] = f_sum[...]
        for k in range(1, DP):
            d_copy(k).wait_recv()
        second_grad[...] = gathered[...]
        value = small_own[zz]
        for k in range(1, 4):
            sz_copy(k).wait_recv()
            value = value + small_z[k]
        small_zsum[...] = value
        for k in range(1, 4):
            sx_copy(k).start()
        for m in range(4):
            pair_copy(m).wait_send()
        for k in range(1, 4):
            for copy in near_copies(k) + far_copies(k):
                copy.wait_send()
            y_copy(k).wait_send()
            sz_copy(k).wait_send()
        for k in range(1, 4):
            sx_copy(k).wait_recv()
            value = value + small_x[k]
        small_sum[...] = value
        for k in range(1, DP):
            e_copy(k).start()
        for k in range(1, DP):
            d_copy(k).wait_send()
        for k in range(1, 4):
            sx_copy(k).wait_send()
        for k in range(1, DP):
            e_copy(k).wait_recv()
            value = value + small_dp[k]
        for k in range(1, DP):
            e_copy(k).wait_send()
        vec_grad[...] = pltpu.roll(value, lax.rem(128 - lax.rem(fs, 4) * SHARD, 128), 1)


def last_kernel(feat_in, second_in, vec_in, feat_out, second_grad, first_grad, *rest):
    *vecs, stage, sems_in, sems_out = rest
    rows = [pl.ds(k * TILE, TILE) for k in range(STEPS)]
    loads = [pltpu.make_async_copy(feat_in.at[:, r], stage.at[:, r], sems_in.at[k]) for k, r in enumerate(rows)]
    stores = [pltpu.make_async_copy(stage.at[:, r], feat_out.at[:, r], sems_out.at[k]) for k, r in enumerate(rows)]
    for copy in loads:
        copy.start()
    for load, store in zip(loads, stores):
        load.wait()
        store.start()
    second_grad[...] = second_in[...]
    first_grad[...] = vec_in[0:TAPS, 0:SHARD]
    for at, ref in enumerate(vecs):
        ref[...] = vec_in[TAPS + at : TAPS + at + 1, 0:SHARD]
    for copy in stores:
        copy.wait()


def whole(shape):
    return pl.BlockSpec(shape, lambda i: (0,) * len(shape))


def local(
    waveforms, packing_list, segment_ids, first_weight, first_bias, first_gain, first_shift,
    second_weight, second_bias, second_gain, second_shift, cotangent,
):
    vecs = (first_bias, first_gain, first_shift, second_bias, second_gain, second_shift)
    vecs = [value.reshape(1, SHARD) for value in vecs]
    shape = jax.ShapeDtypeStruct
    dma = pltpu.SemaphoreType.DMA

    def block(i):
        return (0, jnp.clip(i - 1, 0, STEPS - 1), 0)

    def vmem(kind, *dims):
        return pltpu.VMEM(dims, kind)

    features, second_grad, vec_grad = pl.pallas_call(
        main_kernel,
        grid=(STEPS + 2,),
        out_shape=[shape((1, ROWS, CH), BF16), shape((SHARD, 3 * CH), F32), shape((16, 128), F32)],
        in_specs=[
            whole((4, 128)), whole((1, 128)), whole((320, FRAMES)), whole((TAPS, SHARD)),
            *([whole((1, SHARD))] * 6), whole((SHARD, 3 * CH)), pl.BlockSpec((1, TILE, CH), block),
        ],
        out_specs=[pl.BlockSpec((1, TILE, CH), block), whole((SHARD, 3 * CH)), whole((16, 128))],
        scratch_shapes=[
            vmem(BF16, 128, 320), vmem(BF16, 128, 320), vmem(BF16, 16, 128), vmem(BF16, 4, 16, 128),
            vmem(BF16, 16, 128), vmem(BF16, 4, 16, 128), vmem(BF16, 4, 4, SHARD, 3 * CH), vmem(F32, 144, 384),
            vmem(BF16, 128, CH), vmem(F32, 128, 256), vmem(BF16, TILE + 16, 384), vmem(BF16, 384, 384),
            vmem(BF16, STEPS, 2 * TILE, 128),
            vmem(F32, 16, CH), vmem(BF16, ROWS + 16, CH), vmem(BF16, ROWS, CH), vmem(BF16, ROWS, CH),
            vmem(BF16, ROWS, CH), vmem(BF16, ROWS, 128), vmem(BF16, ROWS, 128), vmem(BF16, ROWS, CH),
            vmem(BF16, ROWS, CH),
            vmem(F32, 8, CH), vmem(F32, CH, 3 * CH), vmem(F32, 24, CH), vmem(F32, TILE, CH), vmem(F32, TILE, CH),
            vmem(BF16, TILE, CH), vmem(BF16, TILE, CH), vmem(BF16, TILE, CH), vmem(BF16, TILE, CH),
            vmem(BF16, 4, 4, 2, 16, 3 * CH),
            vmem(F32, TILE, CH), vmem(F32, TILE, CH), vmem(F32, TILE, CH), vmem(F32, TILE, CH),
            vmem(BF16, 4, 4, 16, 3 * CH), vmem(BF16, 4, 4, 16, 3 * CH),
            vmem(BF16, 4, 4, 16, 768), vmem(BF16, 4, 4, 16, 768),
            vmem(BF16, 4, 16, 768), vmem(BF16, 4, 16, 768), vmem(BF16, 4, 16, 768), vmem(BF16, 4, 16, 768),
            vmem(F32, 16, 3 * CH), vmem(F32, 4, 16, 384), vmem(F32, 16, 384),
            vmem(F32, SHARD, 3 * CH), vmem(BF16, 128, CH), vmem(F32, 128, CH), vmem(F32, 128, 128),
            vmem(F32, 4, 16, 128), vmem(F32, 4, 16, 128), vmem(F32, 16, 128),
            vmem(F32, 4, 16, 128), vmem(F32, 16, 128), vmem(F32, DP, 16, 128),
            dma((DP,)), dma((DP,)), dma((4,)), dma((4,)), dma((4,)), dma((4,)),
            dma((2, 4)), dma((2, 4)), dma((2, 4)), dma((2, 4)), dma, dma,
            dma((4,)), dma((4,)), dma((2, 4)), dma((2, 4)), dma((2, 4)), dma((2, 4)),
            dma((4,)), dma((4,)), dma((DP,)), dma((DP,)),
            dma((4,)), dma((4,)), dma((4,)), dma((4,)), dma((DP,)), dma((DP,)),
        ],
        compiler_params=pltpu.CompilerParams(
            collective_id=0, has_side_effects=True, vmem_limit_bytes=VMEM_LIMIT
        ),
    )(packing_list, segment_ids, waveforms[0].T, first_weight.T, *vecs, second_weight, cotangent)

    one = shape((1, SHARD), F32)
    anywhere = pl.BlockSpec(memory_space=pl.ANY)
    local_vmem = pl.BlockSpec(memory_space=pltpu.VMEM)
    outs = pl.pallas_call(
        last_kernel,
        out_shape=[shape((1, ROWS, CH), BF16), shape((SHARD, 3 * CH), F32), shape((TAPS, SHARD), F32)] + [one] * 6,
        in_specs=[anywhere, local_vmem, local_vmem],
        out_specs=[anywhere] + [local_vmem] * 8,
        scratch_shapes=[pltpu.VMEM((1, ROWS, CH), BF16), dma((STEPS,)), dma((STEPS,))],
        compiler_params=pltpu.CompilerParams(vmem_limit_bytes=VMEM_LIMIT),
    )(features, second_grad, vec_grad)
    b1, n1, s1, b2, n2, s2 = [value.reshape(SHARD) for value in outs[3:]]
    return outs[0], outs[2].T, b1, n1, s1, outs[1], b2, n2, s2


def solution(mesh):
    placed = (
        P("dp", "fsdp", None), P(None, "fsdp"), P("dp", "fsdp"), P("fsdp", None), P("fsdp"), P("fsdp"),
        P("fsdp"), P("fsdp", None), P("fsdp"), P("fsdp"), P("fsdp"), P("dp", "fsdp", None),
    )
    out = (
        P("dp", "fsdp", None), P("fsdp", None), P("fsdp"), P("fsdp"), P("fsdp"), P("fsdp", None),
        P("fsdp"), P("fsdp"), P("fsdp"),
    )
    return jax.shard_map(local, mesh=mesh, in_specs=placed, out_specs=out, check_vma=False)
```

```python
import jax
import jax.numpy as jnp
from jax import lax
from jax.experimental import pallas as pl
from jax.experimental.pallas import tpu as pltpu
from jax.sharding import PartitionSpec as P

MESH = pl.DeviceIdType.MESH
F32, BF16, I32 = jnp.float32, jnp.bfloat16, jnp.int32
EXACT = lax.Precision.HIGHEST
CH, FRAMES, ROWS, TILE, STEPS = 512, 128, 4096, 512, 8
PER_STEP = TILE // 32
PART = 128
VMEM_LIMIT = 60 << 20
DP, FS = 8, 16
SHARD, SLOT, TAPS = 32, 16, 10
EPS = 1e-05
HALF = 0.7071067811865476
EXP_BY = -1.4426950408889634
EXP_PLUS = -0.32574806470870245


def mm(a, b, dims, precision=None):
    return lax.dot_general(
        a, b, (dims, ((), ())), precision=precision, preferred_element_type=F32
    )


def iota(shape, axis):
    return lax.broadcasted_iota(I32, shape, axis)


def patch_mask():
    shape = (TILE + 16, 384)
    lane = iota(shape, 1)
    at = iota(shape, 0) % 32
    first = at * TAPS
    on = (lane >= first) & (lane < first + TAPS) & (lane < 320)
    on |= lane == 320
    on |= (lane == 321) & (at != 31)
    on |= (lane == 322) & (at == 31)
    return jnp.where(on, 1.0, 0.0).astype(BF16)


def patch_pick():
    shape = (384, 384)
    sample = iota(shape, 0)
    out = iota(shape, 1)
    tap = sample - TAPS * ((sample * 6554) // 65536)
    block = out // 128
    lane = out % 128
    group = lane % 16
    within = (lane < 48) & (sample < 320)
    on = (block == 0) & (group < TAPS) & (tap == group)
    on |= (block == 1) & (group < 5) & (tap == group + 5)
    on |= (block == 2) & (group >= 5) & (group < TAPS) & (tap == group - 5)
    on &= within
    flag = (lane == 48) | (lane == 49)
    on |= flag & (block == 0) & (sample == 320)
    on |= flag & (block == 1) & ((sample == 321) | (sample == 322))
    return jnp.where(on, 1.0, 0.0).astype(BF16)


def along_x(fs, k):
    return fs // 4 * 4 + lax.rem(fs + k, 4)


def along_z(fs, k):
    return lax.rem(fs + 4 * k, FS)


def greet(dp, fs):
    barrier = pltpu.get_barrier_semaphore()
    for k in range(1, DP):
        pl.semaphore_signal(barrier, inc=1, device_id=(lax.rem(dp + k, DP), fs), device_id_type=MESH)
    for k in range(1, 4):
        pl.semaphore_signal(barrier, inc=1, device_id=(dp, along_x(fs, k)), device_id_type=MESH)
        pl.semaphore_signal(barrier, inc=1, device_id=(dp, along_z(fs, k)), device_id_type=MESH)


def all_here():
    pl.semaphore_wait(pltpu.get_barrier_semaphore(), DP - 1 + 6)


def send(src, dst, send_sem, recv_sem, device):
    return pltpu.make_async_remote_copy(
        src_ref=src, dst_ref=dst, send_sem=send_sem, recv_sem=recv_sem,
        device_id=device, device_id_type=MESH,
    )


def centred_weights(small):
    centred = small - jnp.mean(small, axis=1, keepdims=True)
    return jnp.where(iota((16, CH), 0) <= TAPS, centred, 0.0)


def split(value):
    high = value.astype(BF16).astype(F32)
    return high, value - high


def weave(*lists):
    queue = []
    for jobs in lists:
        queue += [((at + 0.5) / len(jobs), job) for at, job in enumerate(jobs)]
    for _, job in sorted(queue, key=lambda entry: entry[0]):
        job()


def tile_rows(index):
    return pl.ds(pl.multiple_of(index * TILE, TILE), TILE)


def main_kernel(
    list_ref, seg_ref, wave_ref, weight_ref, vec_0, vec_1, vec_2, vec_3, vec_4, vec_5, second_ref, cot_ref,
    feat_ref, second_grad, vec_grad,
    slots, heard, part_own, smalls, part_row, part_rows, second_all, frames, rhs, quad, mask_ref, pick_ref, patches,
    small_ref, he, ho, de, do, le, lo, g1, gs,
    carry, total, sums_ref, pre_0, pre_1, g_0, g_1, gs_0, gs_1, grad_ref,
    even_0, even_1, odd_0, odd_1, pair_in, pair_sum, near_a, near_b, sum_a, sum_b,
    far_a, far_b, f_all, y_in, f_sum, gathered, wz, t_acc, r_acc,
    small_own, small_z, small_zsum, small_x, small_sum, small_dp,
    a2a_s, a2a_r, sm_s, sm_r, sz_0, sz_1, w_s, w_r, v_s, v_r, fw_s, fw_r,
    p_s, p_r, n_s, n_r, m_s, m_r, y_s, y_r, d_s, d_r, sz_s, sz_r, sx_s, sx_r, e_s, e_r,
):
    step = pl.program_id(0)
    dp, fs = lax.axis_index("dp"), lax.axis_index("fsdp")
    core = lax.rem(dp, 2)
    yy = dp // 2
    zz, xx = fs // 4, lax.rem(fs, 4)
    sibling = dp + 1 - 2 * core
    half = pl.ds(pl.multiple_of(core * 768, 128), 768)
    quarter = pl.ds(pl.multiple_of(yy * 384, 128), 384)
    pres, gs_pair = (pre_0, pre_1), ((g_0, gs_0), (g_1, gs_1))
    spreads = ((even_0, odd_0), (even_1, odd_1))

    def a2a_copy(k):
        target = lax.rem(dp + k, DP)
        return send(
            slots.at[pl.ds(pl.multiple_of(target * SLOT, SLOT), SLOT)],
            heard.at[pl.ds(pl.multiple_of(dp * SLOT, SLOT), SLOT)],
            a2a_s.at[k], a2a_r.at[k], (target, fs),
        )

    w_cols_a = pl.ds(pl.multiple_of(core * 768, 128), 384)
    w_cols_b = pl.ds(pl.multiple_of(core * 768 + 384, 128), 384)

    def part_x(k):
        return send(part_own, smalls.at[k], sm_s.at[k], sm_r.at[k], (dp, along_x(fs, k)))

    def part_z(k):
        return send(part_row, part_rows.at[zz], sz_0.at[k], sz_1.at[k], (dp, along_z(fs, k)))

    def near_weights(k):
        return (
            send(second_ref.at[:, w_cols_a], second_all.at[zz, xx, :, w_cols_a], w_s.at[0, k], w_r.at[0, k], (dp, along_x(fs, k))),
            send(second_ref.at[:, w_cols_b], second_all.at[zz, xx, :, w_cols_b], w_s.at[1, k], w_r.at[1, k], (dp, along_z(fs, k))),
        )

    def far_weights(k):
        piece_a = second_all.at[zz, :, :, w_cols_a]
        piece_b = second_all.at[:, xx, :, w_cols_b]
        return (
            send(piece_a, piece_a, v_s.at[0, k], v_r.at[0, k], (dp, along_z(fs, k))),
            send(piece_b, piece_b, v_s.at[1, k], v_r.at[1, k], (dp, along_x(fs, k))),
        )

    def forward_copy():
        piece = second_all.at[:, :, :, half]
        return send(piece, piece, fw_s, fw_r, (sibling, fs))

    @pl.when(step == 0)
    def _():
        greet(dp, fs)
        sums_ref[...] = jnp.zeros_like(sums_ref)
        carry[...] = jnp.zeros_like(carry)
        total[...] = jnp.zeros_like(total)
        he[ROWS:] = jnp.zeros((16, CH), BF16)
        t_acc[...] = jnp.zeros_like(t_acc)
        r_acc[...] = jnp.zeros_like(r_acc)
        table = list_ref[...].astype(F32)
        eye = iota((128, 128), 0) == iota((128, 128), 1)

        def row(i):
            return jnp.broadcast_to(table[i : i + 1], (128, 128))

        def col(value):
            return jnp.sum(jnp.where(eye, value, 0.0), axis=1, keepdims=True)

        source, owner, place, length = row(0), row(1), row(2), row(3)
        source_c, owner_c, length_c = col(source), col(owner), col(length)
        earlier = (iota((128, 128), 0) < iota((128, 128), 1)) & (source_c == source)
        read_at = jnp.sum(jnp.where(earlier, length_c, 0.0), axis=0, keepdims=True)
        slot_at = jnp.sum(
            jnp.where(earlier & (owner_c == owner), length_c, 0.0), axis=0, keepdims=True
        )
        read_at = jnp.broadcast_to(read_at, (128, 128))
        slot_at = jnp.broadcast_to(slot_at, (128, 128))
        row_at = iota((128, 128), 0)
        lane_f = iota((128, 128), 1).astype(F32)
        group = (row_at // SLOT).astype(F32)
        inner = (row_at % SLOT).astype(F32)
        me = dp.astype(F32)
        entry = (
            (owner == group) & (source == me)
            & (slot_at <= inner) & (inner < slot_at + length)
        )
        frame = jnp.sum(jnp.where(entry, read_at + inner - slot_at + 1.0, 0.0), axis=1, keepdims=True)
        pack = jnp.where(lane_f + 1.0 == frame, 1.0, 0.0).astype(BF16)
        slots[...] = mm(pack, wave_ref[...], ((1,), (1,))).astype(BF16)

        place_lanes = jnp.where(
            iota((SHARD, 128), 1) == iota((SHARD, 128), 0) + lax.rem(fs, 4) * SHARD, 1.0, 0.0
        ).astype(BF16)
        quad[0:TAPS, 0:128] = mm(weight_ref[...], place_lanes, ((1,), (0,)))
        frames[0:8, 0:128] = jnp.zeros((8, 128), F32)
        for at, ref in enumerate((vec_0, vec_1, vec_2, vec_3, vec_4, vec_5)):
            frames[at : at + 1, 0:SHARD] = ref[...].astype(F32)
        vecs = frames[0:8, 0:SHARD].astype(BF16)
        quad[TAPS:16, 0:128] = mm(vecs, place_lanes, ((1,), (0,)))[0:6]
        part_own[...] = quad[0:16, 0:128].astype(BF16)

        all_here()
        for k in range(1, 4):
            part_x(k).start()
        for k in range(1, DP):
            a2a_copy(k).start()
        for k in range(1, 4):
            for copy in near_weights(k):
                copy.start()
        mask_ref[...] = patch_mask()
        whole_row = part_own[...].astype(F32)
        for k in range(1, 4):
            part_x(k).wait_recv()
            whole_row = whole_row + smalls[k].astype(F32)
        part_row[...] = whole_row.astype(BF16)
        for k in range(1, 4):
            part_z(k).start()
        pick_ref[...] = patch_pick()
        mine = pl.ds(pl.multiple_of(dp * SLOT, SLOT), SLOT)
        heard[mine] = slots[mine]
        second_all[zz, xx, :, half] = second_ref[:, half]

        position = row_at.astype(F32)
        entry = (owner == me) & (position >= place) & (position < place + length)
        origin = jnp.sum(
            jnp.where(entry, source * SLOT + slot_at + position - place + 1.0, 0.0),
            axis=1, keepdims=True,
        )
        unpack = jnp.where(lane_f + 1.0 == origin, 1.0, 0.0).astype(BF16)
        seg = jnp.broadcast_to(seg_ref[...].astype(F32), (128, 128))
        following = jnp.where(iota((128, 128), 1) == 127, -1.0, pltpu.roll(seg, 127, 1))
        inside = jnp.where(seg >= 0, 1.0, 0.0)
        inside_c = col(inside)
        kept_c = col(jnp.where(following != seg, 0.0, inside))
        lane = iota((128, 128), 1)
        flags = jnp.where(
            (lane == 64) | (lane == 65), inside_c, jnp.where(lane == 66, kept_c, 0.0)
        )

        for k in range(1, DP):
            a2a_copy(k).wait_recv()
        packed = mm(unpack, heard[...], ((1,), (0,)))
        frames[0:128, 256:384] = flags
        frames[0:128, 0:320] = packed
        frames[128:144, :] = jnp.zeros((16, 384), F32)
        def cut(turn, _):
            few = frames[pl.ds(pl.multiple_of(turn * PER_STEP, PER_STEP), PER_STEP + 8)]
            spread = jnp.broadcast_to(few[:, None], (PER_STEP + 8, 32, 384)).reshape(TILE + 256, 384)
            wide = spread[: TILE + 16].astype(BF16) * mask_ref[...]
            taken = mm(wide, pick_ref[...], ((1,), (0,)))
            even = taken[:TILE, 0:128]
            odd = taken[:TILE, 128:256] + pltpu.roll(taken[:, 256:384], TILE + 15, 0)[:TILE]
            lane1 = iota((1, 128), 1)
            bias_lane = jnp.where((lane1 == 10) | (lane1 == 26) | (lane1 == 42), 1.0, 0.0)
            patches[turn] = (jnp.concatenate([even, odd], axis=0) + bias_lane).astype(BF16)
            return 0

        lax.fori_loop(0, STEPS, cut, 0)
        for k in range(1, 4):
            for copy in near_weights(k):
                copy.wait_recv()
        for k in range(1, 4):
            for copy in far_weights(k):
                copy.start()

        part_rows[pl.ds(zz, 1)] = part_row[...][None]
        for k in range(1, 4):
            part_z(k).wait_recv()
        small = jnp.concatenate([part_rows[g].astype(F32) for g in range(4)], axis=1)
        small_ref[...] = small
        centred = centred_weights(small)
        high, low = split(centred * small[11:12] * HALF)
        shift_high, shift_low = split(small[12:13] * HALF)
        r16 = iota((16, CH), 0)
        shifts = jnp.where(r16 == 0, shift_high, jnp.where(r16 == 1, shift_low, 0.0))
        rhs[...] = jnp.concatenate(
            [high, low, high, shifts, jnp.zeros((64, CH), F32)], axis=0
        ).astype(BF16)
        wide = jnp.concatenate([centred, jnp.zeros((112, CH), F32)], axis=0)
        gram = mm(centred, wide, ((1,), (1,)), EXACT) * (1.0 / CH)
        gram_a, rest = split(gram)
        gram_b, gram_c = split(rest)
        quad[:, 0:128] = jnp.concatenate(
            [gram_a, gram_b, gram_c, jnp.zeros((80, 128), F32)], axis=0
        )
        quad[:, 128:256] = jnp.where(row_at == 48, 1.0, 0.0)

    def first_block(turn, _):
        patch_bf = patches[turn]
        patch = patch_bf.astype(F32)
        form = mm(patch_bf, quad[...].astype(BF16), ((1,), (0,)))
        var = jnp.sum(form[:, 0:128] * patch, axis=1, keepdims=True)
        scale = lax.rsqrt(jnp.maximum(var, 0.0) + EPS) * form[:, 128:256]
        scaled = patch * scale
        high, low = split(scaled)
        lane_t = iota((2 * TILE, 128), 1)
        left = jnp.where(lane_t < 32, high, jnp.where(lane_t < 48, low, patch)).astype(BF16)
        rows = tile_rows(turn)
        for part, (h_ref, d_ref, l_ref) in enumerate(((he, de, le), (ho, do, lo))):
            piece = left[part * TILE : (part + 1) * TILE]
            l_ref[rows] = piece
            u = mm(piece, rhs[...], ((1,), (0,)))
            phi = HALF * lax.erf(u) + HALF
            h_ref[rows] = (u * phi).astype(BF16)
            bell = jnp.exp2(u * u * EXP_BY + EXP_PLUS)
            d_ref[rows] = (phi + u * bell).astype(BF16)
        return 0

    @pl.when(step == 0)
    def _():
        lax.fori_loop(0, 6, first_block, 0)
        for k in range(1, 4):
            for copy in far_weights(k):
                copy.wait_recv()
        forward_copy().start()
        lax.fori_loop(6, STEPS, first_block, 0)
        for k in range(1, DP):
            a2a_copy(k).wait_send()
        for k in range(1, 4):
            part_x(k).wait_send()
            part_z(k).wait_send()
            for copy in near_weights(k) + far_weights(k):
                copy.wait_send()
        forward_copy().wait_recv()
        forward_copy().wait_send()

    def pair_copy(m):
        return send(grad_ref.at[m, :, 1 - core], pair_in.at[m], p_s.at[m], p_r.at[m], (sibling, fs))

    cols_a, cols_b = pl.ds(0, 768), pl.ds(768, 768)

    def near_copies(k):
        z_to, x_to = lax.rem(zz + k, 4), lax.rem(xx + k, 4)
        return (
            send(pair_sum.at[z_to, :, :, cols_a], near_a.at[k], n_s.at[0, k], n_r.at[0, k], (dp, along_z(fs, k))),
            send(pair_sum.at[:, x_to, :, cols_b], near_b.at[k], n_s.at[1, k], n_r.at[1, k], (dp, along_x(fs, k))),
        )

    def far_copies(k):
        z_to, x_to = lax.rem(zz + k, 4), lax.rem(xx + k, 4)
        return (
            send(sum_a.at[x_to], far_a.at[k], m_s.at[0, k], m_r.at[0, k], (dp, along_x(fs, k))),
            send(sum_b.at[z_to], far_b.at[k], m_s.at[1, k], m_r.at[1, k], (dp, along_z(fs, k))),
        )

    def y_copy(k):
        target = lax.rem(yy + k, 4)
        return send(
            f_all.at[:, pl.ds(pl.multiple_of(target * 384, 128), 384)], y_in.at[k],
            y_s.at[k], y_r.at[k], (target * 2 + core, fs),
        )

    def d_copy(k):
        rows = pl.ds(pl.multiple_of(core * 16, 16), 16)
        return send(f_sum, gathered.at[rows, quarter], d_s.at[k], d_r.at[k], (lax.rem(dp + k, DP), fs))

    def sz_copy(k):
        return send(small_own.at[lax.rem(zz + k, 4)], small_z.at[k], sz_s.at[k], sz_r.at[k], (dp, along_z(fs, k)))

    def sx_copy(k):
        return send(small_zsum, small_x.at[k], sx_s.at[k], sx_r.at[k], (dp, along_x(fs, k)))

    def e_copy(k):
        return send(small_sum, small_dp.at[k], e_s.at[k], e_r.at[k], (lax.rem(dp + k, DP), fs))

    def taps(c, n=None):
        if n is None:
            return second_all[:, :, :, c * CH : (c + 1) * CH].reshape(CH, CH)
        return second_all[2 * n : 2 * n + 2, :, :, c * CH : (c + 1) * CH].reshape(CH // 2, CH)

    def convolve(slot):
        rows = tile_rows(step)
        more = pl.ds(pl.multiple_of((step) * TILE, TILE), TILE + 16)
        kept = {}

        def third():
            kept[0] = pltpu.roll(mm(he[more], taps(2), ((1,), (1,))), TILE + 15, 0)[:TILE]

        def first():
            kept[1] = mm(he[rows], taps(0), ((1,), (1,)))

        def rest():
            pres[slot][...] = kept[1] + mm(ho[rows], taps(1), ((1,), (1,))) + kept[0]

        return [third, first, rest]

    def activate(slot):
        bias, gain, shift = small_ref[13:14], small_ref[14:15], small_ref[15:16]
        gain_u, shift_u = gain * HALF, shift * HALF
        state = {"last": carry[0:1]}

        def norms(part):
            rows = pl.ds(part * PART, PART)
            pre = pres[slot][rows] + bias
            centred = pre - jnp.mean(pre, axis=1, keepdims=True)
            var = jnp.mean(centred * centred, axis=1, keepdims=True)
            scale = lax.rsqrt(var + EPS)
            norm = centred * scale
            state[part] = (norm, scale)

        def slopes(part):
            rows = pl.ds(part * PART, PART)
            far = pl.ds(pl.multiple_of((step - 1) * TILE + part * PART, PART), PART)
            keep = lo[far].astype(F32)[:, 48:49]
            norm, scale = state[part]
            u = norm * gain_u + shift_u
            phi = HALF * lax.erf(u) + HALF
            feat_ref[0, rows] = (u * phi * keep).astype(BF16)
            bell = jnp.exp2(u * u * EXP_BY + EXP_PLUS)
            slope = phi + u * bell
            dnorm = cot_ref[0, rows].astype(F32) * (keep * HALF) * slope * gain
            prod = dnorm * norm
            mean_a = jnp.mean(dnorm, axis=1, keepdims=True)
            mean_b = jnp.mean(prod, axis=1, keepdims=True)
            state[part, 1] = (norm, scale, dnorm, prod, mean_a, mean_b)

        def finish(part):
            rows = pl.ds(part * PART, PART)
            far = pl.ds(pl.multiple_of((step - 1) * TILE + part * PART, PART), PART)
            norm, scale, dnorm, prod, mean_a, mean_b = state[part, 1]
            dpre = (dnorm - mean_a - norm * mean_b) * scale
            for at, value in enumerate((dpre, prod, dnorm)):
                sums_ref[at * 8 : at * 8 + 8] += jnp.sum(value.reshape(PART // 8, 8, CH), axis=0)
            here = dpre.astype(BF16)
            g1[far] = here
            gs_pair[slot][0][rows] = here
            rolled = pltpu.roll(dpre, 1, 0)
            rolled = jnp.where(iota((PART, CH), 0) == 0, state["last"], rolled).astype(BF16)
            gs[far] = rolled
            gs_pair[slot][1][rows] = rolled
            state["last"] = dpre[PART - 1 : PART]
            if part == TILE // PART - 1:
                carry[0:1] = state["last"]

        jobs = []
        count = TILE // PART
        for turn in range(count + 2):
            for lag, job in ((0, norms), (1, slopes), (2, finish)):
                if 0 <= turn - lag < count:
                    jobs.append(lambda job=job, part=turn - lag: job(part))
        return jobs

    def weigh(slot):
        g_part, gs_part = gs_pair[slot]
        rows = tile_rows(step - 2)

        def run(c, n):
            left, right = ((g_part, he), (g_part, ho), (gs_part, he))[c]
            cols = slice(n * 256, n * 256 + 256)
            total[:, c * CH + n * 256 : c * CH + n * 256 + 256] += mm(left[...], right[rows, cols], ((0,), (0,)))

        return [lambda c=c, n=n: run(c, n) for c in range(3) for n in range(2)]

    @pl.when(step == 0)
    def _():
        weave(convolve(0))

    @pl.when(step == 1)
    def _():
        weave(convolve(1), activate(0))

    for slot in range(2):

        @pl.when((step >= 2) & (step < STEPS) & (step % 2 == slot))
        def _(slot=slot):
            weave(convolve(slot) + weigh(slot), activate(1 - slot))

    @pl.when(step == STEPS)
    def _():
        weave(weigh(0), activate(1))

    @pl.when(step == STEPS + 1)
    def _():
        weave(weigh(1))
        grad_ref[...] = total[...].astype(BF16).reshape(4, 4, 2, 16, 3 * CH)
        for m in range(4):
            pair_copy(m).start()

    def spread(slot, turn):
        rows = tile_rows(turn)

        kept = {}

        def even(n):
            cols = slice(n * 256, n * 256 + 256)
            kept[n] = mm(g1[rows], taps(0)[:, cols], ((1,), (0,)))

        def more(n):
            cols = slice(n * 256, n * 256 + 256)
            spreads[slot][0][:, cols] = kept[n] + mm(gs[rows], taps(2)[:, cols], ((1,), (0,)))

        def odd(n):
            cols = slice(n * 256, n * 256 + 256)
            spreads[slot][1][:, cols] = mm(g1[rows], taps(1)[:, cols], ((1,), (0,)))

        order = ((even, 0), (more, 0), (even, 1), (more, 1), (odd, 0), (odd, 1))
        return [lambda job=job, n=n: job(n) for job, n in order]

    def gather_terms(slot, turn):
        size = TILE
        lane = iota((size, 128), 1)

        def run(parity, part):
            near = pl.ds(part * size, size)
            rows = pl.ds(pl.multiple_of(turn * TILE + part * size, size), size)
            slope, lhs = ((de, le), (do, lo))[parity]
            ds = (spreads[slot][parity][near] * slope[rows].astype(F32)).astype(BF16)
            left = lhs[rows]
            left_f = left.astype(F32)
            z = mm(ds, wz[...], ((1,), (1,)))
            inner = jnp.where(lane < 48, z * left_f, 0.0)
            corr = jnp.sum(inner, axis=1, keepdims=True)
            y = jnp.where(lane < 48, corr * left_f, z).astype(BF16)
            t_acc[...] += mm(left, ds, ((0,), (0,)))
            r_acc[...] += mm(y, left, ((0,), (0,)))

        return [lambda a=a, b=b: run(a, b) for a in range(2) for b in range(1)]

    @pl.when(step == STEPS + 1)
    def _():
        def both(slot, turn):
            weave(spread(slot, turn), gather_terms(1 - slot, turn - 1))

        def pair(turn, _):
            both(0, 2 * turn)
            both(1, 2 * turn + 1)
            return 0

        small = small_ref[...]
        gain = small[11:12]
        high, low = split(centred_weights(small) * gain)
        wz[...] = jnp.concatenate(
            [high, low, high, jnp.where(iota((16, CH), 0) == 0, gain, 0.0), jnp.zeros((64, CH), F32)], axis=0
        ).astype(BF16)
        weave(spread(0, 0))
        both(1, 1)
        for m in range(4):
            pair_copy(m).wait_recv()
            pair_sum[m] = (grad_ref[m, :, core].astype(F32) + pair_in[m].astype(F32)).astype(BF16)
        for k in range(1, 4):
            for copy in near_copies(k):
                copy.start()
        lax.fori_loop(1, 3, pair, 0)
        value_a = pair_sum[zz, :, :, cols_a].astype(F32)
        value_b = pair_sum[:, xx, :, cols_b].astype(F32)
        for k in range(1, 4):
            for copy in near_copies(k):
                copy.wait_recv()
            value_a = value_a + near_a[k].astype(F32)
            value_b = value_b + near_b[k].astype(F32)
        sum_a[...] = value_a.astype(BF16)
        sum_b[...] = value_b.astype(BF16)
        for k in range(1, 4):
            for copy in far_copies(k):
                copy.start()
        both(0, 6)
        both(1, 7)
        value_a = sum_a[xx].astype(F32)
        value_b = sum_b[zz].astype(F32)
        for k in range(1, 4):
            for copy in far_copies(k):
                copy.wait_recv()
            value_a = value_a + far_a[k].astype(F32)
            value_b = value_b + far_b[k].astype(F32)
        f_all[:, cols_a] = value_a
        f_all[:, cols_b] = value_b
        for k in range(1, 4):
            y_copy(k).start()
        weave(gather_terms(1, STEPS - 1))
        small = small_ref[...]
        centred = centred_weights(small)
        gain = small[11:12]
        r16 = iota((16, CH), 0)
        t_core = t_acc[0:16] + t_acc[32:48]
        r_rows = jnp.concatenate(
            [r_acc[0:16] + r_acc[32:48], jnp.where(iota((8, 128), 0) == 0, r_acc[48:56], 0.0)], axis=0
        )
        r_rows = r_rows + pltpu.roll(r_rows, 96, 1)
        right = jnp.concatenate([centred, jnp.where(iota((8, CH), 0) == 0, 1.0, 0.0)], axis=0)
        corr = mm(r_rows, right, ((0,), (0,)), EXACT)[0:16] * (1.0 / CH)
        grad = (gain * t_core - corr) * HALF
        gain_grad = jnp.sum(centred * t_core, axis=0, keepdims=True) * HALF
        shift_grad = t_acc[48:49] * HALF
        sums = sums_ref[...]
        inv = 1.0 / small[14:15]
        grad = jnp.where(r16 == 11, gain_grad, grad)
        grad = jnp.where(r16 == 12, shift_grad, grad)
        grad = jnp.where(r16 == 13, jnp.sum(sums[0:8], axis=0, keepdims=True), grad)
        grad = jnp.where(r16 == 14, jnp.sum(sums[8:16], axis=0, keepdims=True) * inv, grad)
        grad = jnp.where(r16 == 15, jnp.sum(sums[16:24], axis=0, keepdims=True) * inv, grad)
        for q in range(4):
            small_own[q] = grad[:, q * 128 : (q + 1) * 128]
        for k in range(1, 4):
            sz_copy(k).start()
        value = f_all[:, quarter]
        for k in range(1, 4):
            y_copy(k).wait_recv()
            value = value + y_in[k]
        f_sum[...] = value
        for k in range(1, DP):
            d_copy(k).start()

        rows16 = pl.ds(pl.multiple_of(core * 16, 16), 16)
        gathered[rows16, quarter] = f_sum[...]
        value = small_own[zz]
        for k in range(1, 4):
            sz_copy(k).wait_recv()
            value = value + small_z[k]
        small_zsum[...] = value
        for k in range(1, 4):
            sx_copy(k).start()
        for m in range(4):
            pair_copy(m).wait_send()
        for k in range(1, 4):
            for copy in near_copies(k) + far_copies(k):
                copy.wait_send()
            y_copy(k).wait_send()
            sz_copy(k).wait_send()
        for k in range(1, 4):
            sx_copy(k).wait_recv()
            value = value + small_x[k]
        small_sum[...] = value
        for k in range(1, DP):
            e_copy(k).start()
        for k in range(1, DP):
            d_copy(k).wait_recv()
        second_grad[...] = gathered[...]
        for k in range(1, DP):
            d_copy(k).wait_send()
        for k in range(1, 4):
            sx_copy(k).wait_send()
        for k in range(1, DP):
            e_copy(k).wait_recv()
            value = value + small_dp[k]
        for k in range(1, DP):
            e_copy(k).wait_send()
        vec_grad[...] = pltpu.roll(value, lax.rem(128 - lax.rem(fs, 4) * SHARD, 128), 1)


def last_kernel(feat_in, second_in, vec_in, feat_out, second_grad, first_grad, *rest):
    *vecs, stage, sems_in, sems_out = rest
    rows = [pl.ds(k * TILE, TILE) for k in range(STEPS)]
    loads = [pltpu.make_async_copy(feat_in.at[:, r], stage.at[:, r], sems_in.at[k]) for k, r in enumerate(rows)]
    stores = [pltpu.make_async_copy(stage.at[:, r], feat_out.at[:, r], sems_out.at[k]) for k, r in enumerate(rows)]
    for copy in loads:
        copy.start()
    for load, store in zip(loads, stores):
        load.wait()
        store.start()
    second_grad[...] = second_in[...]
    first_grad[...] = vec_in[0:TAPS, 0:SHARD]
    for at, ref in enumerate(vecs):
        ref[...] = vec_in[TAPS + at : TAPS + at + 1, 0:SHARD]
    for copy in stores:
        copy.wait()


def whole(shape):
    return pl.BlockSpec(shape, lambda i: (0,) * len(shape))


def local(
    waveforms, packing_list, segment_ids, first_weight, first_bias, first_gain, first_shift,
    second_weight, second_bias, second_gain, second_shift, cotangent,
):
    vecs = (first_bias, first_gain, first_shift, second_bias, second_gain, second_shift)
    vecs = [value.reshape(1, SHARD) for value in vecs]
    shape = jax.ShapeDtypeStruct
    dma = pltpu.SemaphoreType.DMA

    def block(i):
        return (0, jnp.clip(i - 1, 0, STEPS - 1), 0)

    def vmem(kind, *dims):
        return pltpu.VMEM(dims, kind)

    features, second_grad, vec_grad = pl.pallas_call(
        main_kernel,
        grid=(STEPS + 2,),
        out_shape=[shape((1, ROWS, CH), BF16), shape((SHARD, 3 * CH), F32), shape((16, 128), F32)],
        in_specs=[
            whole((4, 128)), whole((1, 128)), whole((320, FRAMES)), whole((TAPS, SHARD)),
            *([whole((1, SHARD))] * 6), whole((SHARD, 3 * CH)), pl.BlockSpec((1, TILE, CH), block),
        ],
        out_specs=[pl.BlockSpec((1, TILE, CH), block), whole((SHARD, 3 * CH)), whole((16, 128))],
        scratch_shapes=[
            vmem(BF16, 128, 320), vmem(BF16, 128, 320), vmem(BF16, 16, 128), vmem(BF16, 4, 16, 128),
            vmem(BF16, 16, 128), vmem(BF16, 4, 16, 128), vmem(BF16, 4, 4, SHARD, 3 * CH), vmem(F32, 144, 384),
            vmem(BF16, 128, CH), vmem(F32, 128, 256), vmem(BF16, TILE + 16, 384), vmem(BF16, 384, 384),
            vmem(BF16, STEPS, 2 * TILE, 128),
            vmem(F32, 16, CH), vmem(BF16, ROWS + 16, CH), vmem(BF16, ROWS, CH), vmem(BF16, ROWS, CH),
            vmem(BF16, ROWS, CH), vmem(BF16, ROWS, 128), vmem(BF16, ROWS, 128), vmem(BF16, ROWS, CH),
            vmem(BF16, ROWS, CH),
            vmem(F32, 8, CH), vmem(F32, CH, 3 * CH), vmem(F32, 24, CH), vmem(F32, TILE, CH), vmem(F32, TILE, CH),
            vmem(BF16, TILE, CH), vmem(BF16, TILE, CH), vmem(BF16, TILE, CH), vmem(BF16, TILE, CH),
            vmem(BF16, 4, 4, 2, 16, 3 * CH),
            vmem(F32, TILE, CH), vmem(F32, TILE, CH), vmem(F32, TILE, CH), vmem(F32, TILE, CH),
            vmem(BF16, 4, 4, 16, 3 * CH), vmem(BF16, 4, 4, 16, 3 * CH),
            vmem(BF16, 4, 4, 16, 768), vmem(BF16, 4, 4, 16, 768),
            vmem(BF16, 4, 16, 768), vmem(BF16, 4, 16, 768), vmem(BF16, 4, 16, 768), vmem(BF16, 4, 16, 768),
            vmem(F32, 16, 3 * CH), vmem(F32, 4, 16, 384), vmem(F32, 16, 384),
            vmem(F32, SHARD, 3 * CH), vmem(BF16, 128, CH), vmem(F32, 128, CH), vmem(F32, 128, 128),
            vmem(F32, 4, 16, 128), vmem(F32, 4, 16, 128), vmem(F32, 16, 128),
            vmem(F32, 4, 16, 128), vmem(F32, 16, 128), vmem(F32, DP, 16, 128),
            dma((DP,)), dma((DP,)), dma((4,)), dma((4,)), dma((4,)), dma((4,)),
            dma((2, 4)), dma((2, 4)), dma((2, 4)), dma((2, 4)), dma, dma,
            dma((4,)), dma((4,)), dma((2, 4)), dma((2, 4)), dma((2, 4)), dma((2, 4)),
            dma((4,)), dma((4,)), dma((DP,)), dma((DP,)),
            dma((4,)), dma((4,)), dma((4,)), dma((4,)), dma((DP,)), dma((DP,)),
        ],
        compiler_params=pltpu.CompilerParams(
            collective_id=0, has_side_effects=True, vmem_limit_bytes=VMEM_LIMIT
        ),
    )(packing_list, segment_ids, waveforms[0].T, first_weight.T, *vecs, second_weight, cotangent)

    one = shape((1, SHARD), F32)
    anywhere = pl.BlockSpec(memory_space=pl.ANY)
    local_vmem = pl.BlockSpec(memory_space=pltpu.VMEM)
    outs = pl.pallas_call(
        last_kernel,
        out_shape=[shape((1, ROWS, CH), BF16), shape((SHARD, 3 * CH), F32), shape((TAPS, SHARD), F32)] + [one] * 6,
        in_specs=[anywhere, local_vmem, local_vmem],
        out_specs=[anywhere] + [local_vmem] * 8,
        scratch_shapes=[pltpu.VMEM((1, ROWS, CH), BF16), dma((STEPS,)), dma((STEPS,))],
        compiler_params=pltpu.CompilerParams(vmem_limit_bytes=VMEM_LIMIT),
    )(features, second_grad, vec_grad)
    b1, n1, s1, b2, n2, s2 = [value.reshape(SHARD) for value in outs[3:]]
    return outs[0], outs[2].T, b1, n1, s1, outs[1], b2, n2, s2


def solution(mesh):
    placed = (
        P("dp", "fsdp", None), P(None, "fsdp"), P("dp", "fsdp"), P("fsdp", None), P("fsdp"), P("fsdp"),
        P("fsdp"), P("fsdp", None), P("fsdp"), P("fsdp"), P("fsdp"), P("dp", "fsdp", None),
    )
    out = (
        P("dp", "fsdp", None), P("fsdp", None), P("fsdp"), P("fsdp"), P("fsdp"), P("fsdp", None),
        P("fsdp"), P("fsdp"), P("fsdp"),
    )
    return jax.shard_map(local, mesh=mesh, in_specs=placed, out_specs=out, check_vma=False)
```

```python
import jax
import jax.numpy as jnp
from jax import lax
from jax.experimental import pallas as pl
from jax.experimental.pallas import tpu as pltpu
from jax.sharding import PartitionSpec as P

MESH = pl.DeviceIdType.MESH
F32, BF16, I32 = jnp.float32, jnp.bfloat16, jnp.int32
EXACT = lax.Precision.HIGHEST
CH, FRAMES, ROWS, TILE, STEPS = 512, 128, 4096, 512, 8
PER_STEP = TILE // 32
PART = 128
VMEM_LIMIT = 60 << 20
DP, FS = 8, 16
SHARD, SLOT, TAPS = 32, 16, 10
EPS = 1e-05
HALF = 0.7071067811865476
EXP_BY = -1.4426950408889634
EXP_PLUS = -0.32574806470870245


def mm(a, b, dims, precision=None):
    return lax.dot_general(
        a, b, (dims, ((), ())), precision=precision, preferred_element_type=F32
    )


def iota(shape, axis):
    return lax.broadcasted_iota(I32, shape, axis)


def patch_mask():
    shape = (TILE + 16, 384)
    lane = iota(shape, 1)
    at = iota(shape, 0) % 32
    first = at * TAPS
    on = (lane >= first) & (lane < first + TAPS) & (lane < 320)
    on |= lane == 320
    on |= (lane == 321) & (at != 31)
    on |= (lane == 322) & (at == 31)
    return jnp.where(on, 1.0, 0.0).astype(BF16)


def patch_pick():
    shape = (384, 384)
    sample = iota(shape, 0)
    out = iota(shape, 1)
    tap = sample - TAPS * ((sample * 6554) // 65536)
    block = out // 128
    lane = out % 128
    group = lane % 16
    within = (lane < 48) & (sample < 320)
    on = (block == 0) & (group < TAPS) & (tap == group)
    on |= (block == 1) & (group < 5) & (tap == group + 5)
    on |= (block == 2) & (group >= 5) & (group < TAPS) & (tap == group - 5)
    on &= within
    flag = (lane == 48) | (lane == 49)
    on |= flag & (block == 0) & (sample == 320)
    on |= flag & (block == 1) & ((sample == 321) | (sample == 322))
    return jnp.where(on, 1.0, 0.0).astype(BF16)


def along_x(fs, k):
    return fs // 4 * 4 + lax.rem(fs + k, 4)


def along_z(fs, k):
    return lax.rem(fs + 4 * k, FS)


def greet(dp, fs):
    barrier = pltpu.get_barrier_semaphore()
    for k in range(1, DP):
        pl.semaphore_signal(barrier, inc=1, device_id=(lax.rem(dp + k, DP), fs), device_id_type=MESH)
    for k in range(1, 4):
        pl.semaphore_signal(barrier, inc=1, device_id=(dp, along_x(fs, k)), device_id_type=MESH)
        pl.semaphore_signal(barrier, inc=1, device_id=(dp, along_z(fs, k)), device_id_type=MESH)


def all_here():
    pl.semaphore_wait(pltpu.get_barrier_semaphore(), DP - 1 + 6)


def send(src, dst, send_sem, recv_sem, device):
    return pltpu.make_async_remote_copy(
        src_ref=src, dst_ref=dst, send_sem=send_sem, recv_sem=recv_sem,
        device_id=device, device_id_type=MESH,
    )


def centred_weights(small):
    centred = small - jnp.mean(small, axis=1, keepdims=True)
    return jnp.where(iota((16, CH), 0) <= TAPS, centred, 0.0)


def split(value):
    high = value.astype(BF16).astype(F32)
    return high, value - high


def weave(*lists):
    queue = []
    for jobs in lists:
        queue += [((at + 0.5) / len(jobs), job) for at, job in enumerate(jobs)]
    for _, job in sorted(queue, key=lambda entry: entry[0]):
        job()


def tile_rows(index):
    return pl.ds(pl.multiple_of(index * TILE, TILE), TILE)


def main_kernel(
    list_ref, seg_ref, wave_ref, weight_ref, vec_0, vec_1, vec_2, vec_3, vec_4, vec_5, second_ref, cot_ref,
    feat_ref, second_grad, vec_grad,
    slots, heard, part_own, smalls, part_row, part_rows, second_all, frames, rhs, quad, mask_ref, pick_ref, patches,
    small_ref, he, ho, de, do, le, lo, g1, gs,
    carry, total, sums_ref, pre_0, pre_1, g_0, g_1, gs_0, gs_1, grad_ref,
    even_1, odd_1, pair_in, pair_sum, near_a, near_b, sum_a, sum_b,
    far_a, far_b, f_all, y_in, f_sum, gathered, wz, t_acc, r_acc,
    small_own, small_z, small_zsum, small_x, small_sum, small_dp,
    a2a_s, a2a_r, sm_s, sm_r, sz_0, sz_1, w_s, w_r, v_s, v_r, fw_s, fw_r,
    p_s, p_r, n_s, n_r, m_s, m_r, y_s, y_r, d_s, d_r, sz_s, sz_r, sx_s, sx_r, e_s, e_r,
):
    step = pl.program_id(0)
    dp, fs = lax.axis_index("dp"), lax.axis_index("fsdp")
    core = lax.rem(dp, 2)
    yy = dp // 2
    zz, xx = fs // 4, lax.rem(fs, 4)
    sibling = dp + 1 - 2 * core
    half = pl.ds(pl.multiple_of(core * 768, 128), 768)
    quarter = pl.ds(pl.multiple_of(yy * 384, 128), 384)
    pres, gs_pair = (pre_0, pre_1), ((g_0, gs_0), (g_1, gs_1))
    spreads = ((pre_0, pre_1), (even_1, odd_1))

    def a2a_copy(k):
        target = lax.rem(dp + k, DP)
        return send(
            slots.at[pl.ds(pl.multiple_of(target * SLOT, SLOT), SLOT)],
            heard.at[pl.ds(pl.multiple_of(dp * SLOT, SLOT), SLOT)],
            a2a_s.at[k], a2a_r.at[k], (target, fs),
        )

    w_cols_a = pl.ds(pl.multiple_of(core * 768, 128), 384)
    w_cols_b = pl.ds(pl.multiple_of(core * 768 + 384, 128), 384)

    def part_x(k):
        return send(part_own, smalls.at[k], sm_s.at[k], sm_r.at[k], (dp, along_x(fs, k)))

    def part_z(k):
        return send(part_row, part_rows.at[zz], sz_0.at[k], sz_1.at[k], (dp, along_z(fs, k)))

    def near_weights(k):
        return (
            send(second_ref.at[:, w_cols_a], second_all.at[zz, xx, :, w_cols_a], w_s.at[0, k], w_r.at[0, k], (dp, along_x(fs, k))),
            send(second_ref.at[:, w_cols_b], second_all.at[zz, xx, :, w_cols_b], w_s.at[1, k], w_r.at[1, k], (dp, along_z(fs, k))),
        )

    def far_weights(k):
        piece_a = second_all.at[zz, :, :, w_cols_a]
        piece_b = second_all.at[:, xx, :, w_cols_b]
        return (
            send(piece_a, piece_a, v_s.at[0, k], v_r.at[0, k], (dp, along_z(fs, k))),
            send(piece_b, piece_b, v_s.at[1, k], v_r.at[1, k], (dp, along_x(fs, k))),
        )

    def forward_copy():
        piece = second_all.at[:, :, :, half]
        return send(piece, piece, fw_s, fw_r, (sibling, fs))

    @pl.when(step == 0)
    def _():
        greet(dp, fs)
        sums_ref[...] = jnp.zeros_like(sums_ref)
        carry[...] = jnp.zeros_like(carry)
        total[...] = jnp.zeros_like(total)
        he[ROWS:] = jnp.zeros((16, CH), BF16)
        t_acc[...] = jnp.zeros_like(t_acc)
        r_acc[...] = jnp.zeros_like(r_acc)
        table = list_ref[...].astype(F32)
        eye = iota((128, 128), 0) == iota((128, 128), 1)

        def row(i):
            return jnp.broadcast_to(table[i : i + 1], (128, 128))

        def col(value):
            return jnp.sum(jnp.where(eye, value, 0.0), axis=1, keepdims=True)

        source, owner, place, length = row(0), row(1), row(2), row(3)
        source_c, owner_c, length_c = col(source), col(owner), col(length)
        earlier = (iota((128, 128), 0) < iota((128, 128), 1)) & (source_c == source)
        read_at = jnp.sum(jnp.where(earlier, length_c, 0.0), axis=0, keepdims=True)
        slot_at = jnp.sum(
            jnp.where(earlier & (owner_c == owner), length_c, 0.0), axis=0, keepdims=True
        )
        read_at = jnp.broadcast_to(read_at, (128, 128))
        slot_at = jnp.broadcast_to(slot_at, (128, 128))
        row_at = iota((128, 128), 0)
        lane_f = iota((128, 128), 1).astype(F32)
        group = (row_at // SLOT).astype(F32)
        inner = (row_at % SLOT).astype(F32)
        me = dp.astype(F32)
        entry = (
            (owner == group) & (source == me)
            & (slot_at <= inner) & (inner < slot_at + length)
        )
        frame = jnp.sum(jnp.where(entry, read_at + inner - slot_at + 1.0, 0.0), axis=1, keepdims=True)
        pack = jnp.where(lane_f + 1.0 == frame, 1.0, 0.0).astype(BF16)
        slots[...] = mm(pack, wave_ref[...], ((1,), (1,))).astype(BF16)

        place_lanes = jnp.where(
            iota((SHARD, 128), 1) == iota((SHARD, 128), 0) + lax.rem(fs, 4) * SHARD, 1.0, 0.0
        ).astype(BF16)
        quad[0:TAPS, 0:128] = mm(weight_ref[...], place_lanes, ((1,), (0,)))
        frames[0:8, 0:128] = jnp.zeros((8, 128), F32)
        for at, ref in enumerate((vec_0, vec_1, vec_2, vec_3, vec_4, vec_5)):
            frames[at : at + 1, 0:SHARD] = ref[...].astype(F32)
        vecs = frames[0:8, 0:SHARD].astype(BF16)
        quad[TAPS:16, 0:128] = mm(vecs, place_lanes, ((1,), (0,)))[0:6]
        part_own[...] = quad[0:16, 0:128].astype(BF16)

        all_here()
        for k in range(1, 4):
            part_x(k).start()
        for k in range(1, DP):
            a2a_copy(k).start()
        for k in range(1, 4):
            for copy in near_weights(k):
                copy.start()
        mask_ref[...] = patch_mask()
        whole_row = part_own[...].astype(F32)
        for k in range(1, 4):
            part_x(k).wait_recv()
            whole_row = whole_row + smalls[k].astype(F32)
        part_row[...] = whole_row.astype(BF16)
        for k in range(1, 4):
            part_z(k).start()
        pick_ref[...] = patch_pick()
        mine = pl.ds(pl.multiple_of(dp * SLOT, SLOT), SLOT)
        heard[mine] = slots[mine]
        second_all[zz, xx, :, half] = second_ref[:, half]

        position = row_at.astype(F32)
        entry = (owner == me) & (position >= place) & (position < place + length)
        origin = jnp.sum(
            jnp.where(entry, source * SLOT + slot_at + position - place + 1.0, 0.0),
            axis=1, keepdims=True,
        )
        unpack = jnp.where(lane_f + 1.0 == origin, 1.0, 0.0).astype(BF16)
        seg = jnp.broadcast_to(seg_ref[...].astype(F32), (128, 128))
        following = jnp.where(iota((128, 128), 1) == 127, -1.0, pltpu.roll(seg, 127, 1))
        inside = jnp.where(seg >= 0, 1.0, 0.0)
        inside_c = col(inside)
        kept_c = col(jnp.where(following != seg, 0.0, inside))
        lane = iota((128, 128), 1)
        flags = jnp.where(
            (lane == 64) | (lane == 65), inside_c, jnp.where(lane == 66, kept_c, 0.0)
        )

        for k in range(1, DP):
            a2a_copy(k).wait_recv()
        packed = mm(unpack, heard[...], ((1,), (0,)))
        frames[0:128, 256:384] = flags
        frames[0:128, 0:320] = packed
        frames[128:144, :] = jnp.zeros((16, 384), F32)
        def cut(turn, _):
            few = frames[pl.ds(pl.multiple_of(turn * PER_STEP, PER_STEP), PER_STEP + 8)]
            spread = jnp.broadcast_to(few[:, None], (PER_STEP + 8, 32, 384)).reshape(TILE + 256, 384)
            wide = spread[: TILE + 16].astype(BF16) * mask_ref[...]
            taken = mm(wide, pick_ref[...], ((1,), (0,)))
            even = taken[:TILE, 0:128]
            odd = taken[:TILE, 128:256] + pltpu.roll(taken[:, 256:384], TILE + 15, 0)[:TILE]
            lane1 = iota((1, 128), 1)
            bias_lane = jnp.where((lane1 == 10) | (lane1 == 26) | (lane1 == 42), 1.0, 0.0)
            patches[turn] = (jnp.concatenate([even, odd], axis=0) + bias_lane).astype(BF16)
            return 0

        lax.fori_loop(0, STEPS, cut, 0, unroll=2)
        for k in range(1, 4):
            for copy in near_weights(k):
                copy.wait_recv()
        for k in range(1, 4):
            for copy in far_weights(k):
                copy.start()

        part_rows[pl.ds(zz, 1)] = part_row[...][None]
        for k in range(1, 4):
            part_z(k).wait_recv()
        small = jnp.concatenate([part_rows[g].astype(F32) for g in range(4)], axis=1)
        small_ref[...] = small
        centred = centred_weights(small)
        high, low = split(centred * small[11:12] * HALF)
        shift_high, shift_low = split(small[12:13] * HALF)
        r16 = iota((16, CH), 0)
        shifts = jnp.where(r16 == 0, shift_high, jnp.where(r16 == 1, shift_low, 0.0))
        rhs[...] = jnp.concatenate(
            [high, low, high, shifts, jnp.zeros((64, CH), F32)], axis=0
        ).astype(BF16)
        wide = jnp.concatenate([centred, jnp.zeros((112, CH), F32)], axis=0)
        gram = mm(centred, wide, ((1,), (1,)), EXACT) * (1.0 / CH)
        gram_a, rest = split(gram)
        gram_b, gram_c = split(rest)
        quad[:, 0:128] = jnp.concatenate(
            [gram_a, gram_b, gram_c, jnp.zeros((80, 128), F32)], axis=0
        )
        quad[:, 128:256] = jnp.where(row_at == 48, 1.0, 0.0)

    def first_block(turn, _):
        patch_bf = patches[turn]
        patch = patch_bf.astype(F32)
        form = mm(patch_bf, quad[...].astype(BF16), ((1,), (0,)))
        var = jnp.sum(form[:, 0:128] * patch, axis=1, keepdims=True)
        scale = lax.rsqrt(jnp.maximum(var, 0.0) + EPS) * form[:, 128:256]
        scaled = patch * scale
        high, low = split(scaled)
        lane_t = iota((2 * TILE, 128), 1)
        left = jnp.where(lane_t < 32, high, jnp.where(lane_t < 48, low, patch)).astype(BF16)
        rows = tile_rows(turn)
        for part, (h_ref, d_ref, l_ref) in enumerate(((he, de, le), (ho, do, lo))):
            piece = left[part * TILE : (part + 1) * TILE]
            l_ref[rows] = piece
            u = mm(piece, rhs[...], ((1,), (0,)))
            phi = HALF * lax.erf(u) + HALF
            h_ref[rows] = (u * phi).astype(BF16)
            bell = jnp.exp2(u * u * EXP_BY + EXP_PLUS)
            d_ref[rows] = (phi + u * bell).astype(BF16)
        return 0

    @pl.when(step == 0)
    def _():
        lax.fori_loop(0, 6, first_block, 0, unroll=2)
        for k in range(1, 4):
            for copy in far_weights(k):
                copy.wait_recv()
        forward_copy().start()
        lax.fori_loop(6, STEPS, first_block, 0, unroll=2)
        for k in range(1, DP):
            a2a_copy(k).wait_send()
        for k in range(1, 4):
            part_x(k).wait_send()
            part_z(k).wait_send()
            for copy in near_weights(k) + far_weights(k):
                copy.wait_send()
        forward_copy().wait_recv()
        forward_copy().wait_send()

    def pair_copy(m):
        return send(grad_ref.at[m, :, 1 - core], pair_in.at[m], p_s.at[m], p_r.at[m], (sibling, fs))

    cols_a, cols_b = pl.ds(0, 768), pl.ds(768, 768)

    def near_copies(k):
        z_to, x_to = lax.rem(zz + k, 4), lax.rem(xx + k, 4)
        return (
            send(pair_sum.at[z_to, :, :, cols_a], near_a.at[k], n_s.at[0, k], n_r.at[0, k], (dp, along_z(fs, k))),
            send(pair_sum.at[:, x_to, :, cols_b], near_b.at[k], n_s.at[1, k], n_r.at[1, k], (dp, along_x(fs, k))),
        )

    def far_copies(k):
        z_to, x_to = lax.rem(zz + k, 4), lax.rem(xx + k, 4)
        return (
            send(sum_a.at[x_to], far_a.at[k], m_s.at[0, k], m_r.at[0, k], (dp, along_x(fs, k))),
            send(sum_b.at[z_to], far_b.at[k], m_s.at[1, k], m_r.at[1, k], (dp, along_z(fs, k))),
        )

    def y_copy(k):
        target = lax.rem(yy + k, 4)
        return send(
            f_all.at[:, pl.ds(pl.multiple_of(target * 384, 128), 384)], y_in.at[k],
            y_s.at[k], y_r.at[k], (target * 2 + core, fs),
        )

    def d_copy(k):
        rows = pl.ds(pl.multiple_of(core * 16, 16), 16)
        return send(f_sum, gathered.at[rows, quarter], d_s.at[k], d_r.at[k], (lax.rem(dp + k, DP), fs))

    def sz_copy(k):
        return send(small_own.at[lax.rem(zz + k, 4)], small_z.at[k], sz_s.at[k], sz_r.at[k], (dp, along_z(fs, k)))

    def sx_copy(k):
        return send(small_zsum, small_x.at[k], sx_s.at[k], sx_r.at[k], (dp, along_x(fs, k)))

    def e_copy(k):
        return send(small_sum, small_dp.at[k], e_s.at[k], e_r.at[k], (lax.rem(dp + k, DP), fs))

    def taps(c, n=None):
        if n is None:
            return second_all[:, :, :, c * CH : (c + 1) * CH].reshape(CH, CH)
        return second_all[2 * n : 2 * n + 2, :, :, c * CH : (c + 1) * CH].reshape(CH // 2, CH)

    def convolve(slot):
        rows = tile_rows(step)
        more = pl.ds(pl.multiple_of((step) * TILE, TILE), TILE + 16)
        kept = {}

        def third():
            kept[0] = pltpu.roll(mm(he[more], taps(2), ((1,), (1,))), TILE + 15, 0)[:TILE]

        def first():
            kept[1] = mm(he[rows], taps(0), ((1,), (1,)))

        def rest():
            pres[slot][...] = kept[1] + mm(ho[rows], taps(1), ((1,), (1,))) + kept[0]

        return [third, first, rest]

    def activate(slot):
        bias, gain, shift = small_ref[13:14], small_ref[14:15], small_ref[15:16]
        gain_u, shift_u = gain * HALF, shift * HALF
        state = {"last": carry[0:1]}

        def norms(part):
            rows = pl.ds(part * PART, PART)
            pre = pres[slot][rows] + bias
            centred = pre - jnp.mean(pre, axis=1, keepdims=True)
            var = jnp.mean(centred * centred, axis=1, keepdims=True)
            scale = lax.rsqrt(var + EPS)
            norm = centred * scale
            state[part] = (norm, scale)

        def slopes(part):
            rows = pl.ds(part * PART, PART)
            far = pl.ds(pl.multiple_of((step - 1) * TILE + part * PART, PART), PART)
            keep = lo[far].astype(F32)[:, 48:49]
            norm, scale = state[part]
            u = norm * gain_u + shift_u
            phi = HALF * lax.erf(u) + HALF
            feat_ref[0, rows] = (u * phi * keep).astype(BF16)
            bell = jnp.exp2(u * u * EXP_BY + EXP_PLUS)
            slope = phi + u * bell
            dnorm = cot_ref[0, rows].astype(F32) * (keep * HALF) * slope * gain
            prod = dnorm * norm
            mean_a = jnp.mean(dnorm, axis=1, keepdims=True)
            mean_b = jnp.mean(prod, axis=1, keepdims=True)
            state[part, 1] = (norm, scale, dnorm, prod, mean_a, mean_b)

        def finish(part):
            rows = pl.ds(part * PART, PART)
            far = pl.ds(pl.multiple_of((step - 1) * TILE + part * PART, PART), PART)
            norm, scale, dnorm, prod, mean_a, mean_b = state[part, 1]
            dpre = (dnorm - mean_a - norm * mean_b) * scale
            for at, value in enumerate((dpre, prod, dnorm)):
                sums_ref[at * 8 : at * 8 + 8] += jnp.sum(value.reshape(PART // 8, 8, CH), axis=0)
            here = dpre.astype(BF16)
            g1[far] = here
            gs_pair[slot][0][rows] = here
            rolled = pltpu.roll(dpre, 1, 0)
            rolled = jnp.where(iota((PART, CH), 0) == 0, state["last"], rolled).astype(BF16)
            gs[far] = rolled
            gs_pair[slot][1][rows] = rolled
            state["last"] = dpre[PART - 1 : PART]
            if part == TILE // PART - 1:
                carry[0:1] = state["last"]

        jobs = []
        count = TILE // PART
        for turn in range(count + 2):
            for lag, job in ((0, norms), (1, slopes), (2, finish)):
                if 0 <= turn - lag < count:
                    jobs.append(lambda job=job, part=turn - lag: job(part))
        return jobs

    def weigh(slot):
        g_part, gs_part = gs_pair[slot]
        rows = tile_rows(step - 2)

        def run(c, n):
            left, right = ((g_part, he), (g_part, ho), (gs_part, he))[c]
            cols = slice(n * 256, n * 256 + 256)
            total[:, c * CH + n * 256 : c * CH + n * 256 + 256] += mm(left[...], right[rows, cols], ((0,), (0,)))

        return [lambda c=c, n=n: run(c, n) for c in range(3) for n in range(2)]

    @pl.when(step == 0)
    def _():
        weave(convolve(0))

    @pl.when(step == 1)
    def _():
        weave(convolve(1), activate(0))

    for slot in range(2):

        @pl.when((step >= 2) & (step < STEPS) & (step % 2 == slot))
        def _(slot=slot):
            weave(convolve(slot) + weigh(slot), activate(1 - slot))

    @pl.when(step == STEPS)
    def _():
        weave(weigh(0), activate(1))

    @pl.when(step == STEPS + 1)
    def _():
        weave(weigh(1))
        grad_ref[...] = total[...].astype(BF16).reshape(4, 4, 2, 16, 3 * CH)
        for m in range(4):
            pair_copy(m).start()

    def spread(slot, turn):
        rows = tile_rows(turn)

        kept = {}

        def even(n):
            cols = slice(n * 256, n * 256 + 256)
            kept[n] = mm(g1[rows], taps(0)[:, cols], ((1,), (0,)))

        def more(n):
            cols = slice(n * 256, n * 256 + 256)
            spreads[slot][0][:, cols] = kept[n] + mm(gs[rows], taps(2)[:, cols], ((1,), (0,)))

        def odd(n):
            cols = slice(n * 256, n * 256 + 256)
            spreads[slot][1][:, cols] = mm(g1[rows], taps(1)[:, cols], ((1,), (0,)))

        order = ((even, 0), (more, 0), (even, 1), (more, 1), (odd, 0), (odd, 1))
        return [lambda job=job, n=n: job(n) for job, n in order]

    def gather_terms(slot, turn):
        size = TILE
        lane = iota((size, 128), 1)

        def run(parity, part):
            near = pl.ds(part * size, size)
            rows = pl.ds(pl.multiple_of(turn * TILE + part * size, size), size)
            slope, lhs = ((de, le), (do, lo))[parity]
            ds = (spreads[slot][parity][near] * slope[rows].astype(F32)).astype(BF16)
            left = lhs[rows]
            left_f = left.astype(F32)
            z = mm(ds, wz[...], ((1,), (1,)))
            inner = jnp.where(lane < 48, z * left_f, 0.0)
            corr = jnp.sum(inner, axis=1, keepdims=True)
            y = jnp.where(lane < 48, corr * left_f, z).astype(BF16)
            t_acc[...] += mm(left, ds, ((0,), (0,)))
            r_acc[...] += mm(y, left, ((0,), (0,)))

        return [lambda a=a, b=b: run(a, b) for a in range(2) for b in range(1)]

    @pl.when(step == STEPS + 1)
    def _():
        def both(slot, turn):
            weave(spread(slot, turn), gather_terms(1 - slot, turn - 1))

        def pair(turn, _):
            both(0, 2 * turn)
            both(1, 2 * turn + 1)
            return 0

        small = small_ref[...]
        gain = small[11:12]
        high, low = split(centred_weights(small) * gain)
        wz[...] = jnp.concatenate(
            [high, low, high, jnp.where(iota((16, CH), 0) == 0, gain, 0.0), jnp.zeros((64, CH), F32)], axis=0
        ).astype(BF16)
        weave(spread(0, 0))
        both(1, 1)
        for m in range(4):
            pair_copy(m).wait_recv()
            pair_sum[m] = (grad_ref[m, :, core].astype(F32) + pair_in[m].astype(F32)).astype(BF16)
        for k in range(1, 4):
            for copy in near_copies(k):
                copy.start()
        lax.fori_loop(1, 3, pair, 0)
        value_a = pair_sum[zz, :, :, cols_a].astype(F32)
        value_b = pair_sum[:, xx, :, cols_b].astype(F32)
        for k in range(1, 4):
            for copy in near_copies(k):
                copy.wait_recv()
            value_a = value_a + near_a[k].astype(F32)
            value_b = value_b + near_b[k].astype(F32)
        sum_a[...] = value_a.astype(BF16)
        sum_b[...] = value_b.astype(BF16)
        for k in range(1, 4):
            for copy in far_copies(k):
                copy.start()
        both(0, 6)
        both(1, 7)
        value_a = sum_a[xx].astype(F32)
        value_b = sum_b[zz].astype(F32)
        for k in range(1, 4):
            for copy in far_copies(k):
                copy.wait_recv()
            value_a = value_a + far_a[k].astype(F32)
            value_b = value_b + far_b[k].astype(F32)
        f_all[:, cols_a] = value_a
        f_all[:, cols_b] = value_b
        for k in range(1, 4):
            y_copy(k).start()
        weave(gather_terms(1, STEPS - 1))
        small = small_ref[...]
        centred = centred_weights(small)
        gain = small[11:12]
        r16 = iota((16, CH), 0)
        t_core = t_acc[0:16] + t_acc[32:48]
        r_rows = jnp.concatenate(
            [r_acc[0:16] + r_acc[32:48], jnp.where(iota((8, 128), 0) == 0, r_acc[48:56], 0.0)], axis=0
        )
        r_rows = r_rows + pltpu.roll(r_rows, 96, 1)
        right = jnp.concatenate([centred, jnp.where(iota((8, CH), 0) == 0, 1.0, 0.0)], axis=0)
        corr = mm(r_rows, right, ((0,), (0,)), EXACT)[0:16] * (1.0 / CH)
        grad = (gain * t_core - corr) * HALF
        gain_grad = jnp.sum(centred * t_core, axis=0, keepdims=True) * HALF
        shift_grad = t_acc[48:49] * HALF
        sums = sums_ref[...]
        inv = 1.0 / small[14:15]
        grad = jnp.where(r16 == 11, gain_grad, grad)
        grad = jnp.where(r16 == 12, shift_grad, grad)
        grad = jnp.where(r16 == 13, jnp.sum(sums[0:8], axis=0, keepdims=True), grad)
        grad = jnp.where(r16 == 14, jnp.sum(sums[8:16], axis=0, keepdims=True) * inv, grad)
        grad = jnp.where(r16 == 15, jnp.sum(sums[16:24], axis=0, keepdims=True) * inv, grad)
        for q in range(4):
            small_own[q] = grad[:, q * 128 : (q + 1) * 128]
        for k in range(1, 4):
            sz_copy(k).start()
        value = f_all[:, quarter]
        for k in range(1, 4):
            y_copy(k).wait_recv()
            value = value + y_in[k]
        f_sum[...] = value
        for k in range(1, DP):
            d_copy(k).start()

        rows16 = pl.ds(pl.multiple_of(core * 16, 16), 16)
        gathered[rows16, quarter] = f_sum[...]
        value = small_own[zz]
        for k in range(1, 4):
            sz_copy(k).wait_recv()
            value = value + small_z[k]
        small_zsum[...] = value
        for k in range(1, 4):
            sx_copy(k).start()
        for m in range(4):
            pair_copy(m).wait_send()
        for k in range(1, 4):
            for copy in near_copies(k) + far_copies(k):
                copy.wait_send()
            y_copy(k).wait_send()
            sz_copy(k).wait_send()
        for k in range(1, 4):
            sx_copy(k).wait_recv()
            value = value + small_x[k]
        small_sum[...] = value
        for k in range(1, DP):
            e_copy(k).start()
        for k in range(1, DP):
            d_copy(k).wait_recv()
        second_grad[...] = gathered[...]
        for k in range(1, DP):
            d_copy(k).wait_send()
        for k in range(1, 4):
            sx_copy(k).wait_send()
        for k in range(1, DP):
            e_copy(k).wait_recv()
            value = value + small_dp[k]
        for k in range(1, DP):
            e_copy(k).wait_send()
        vec_grad[...] = pltpu.roll(value, lax.rem(128 - lax.rem(fs, 4) * SHARD, 128), 1)


def last_kernel(feat_in, second_in, vec_in, feat_out, second_grad, first_grad, *rest):
    *vecs, stage, sems_in, sems_out = rest
    rows = [pl.ds(k * TILE, TILE) for k in range(STEPS)]
    loads = [pltpu.make_async_copy(feat_in.at[:, r], stage.at[:, r], sems_in.at[k]) for k, r in enumerate(rows)]
    stores = [pltpu.make_async_copy(stage.at[:, r], feat_out.at[:, r], sems_out.at[k]) for k, r in enumerate(rows)]
    for copy in loads:
        copy.start()
    for load, store in zip(loads, stores):
        load.wait()
        store.start()
    second_grad[...] = second_in[...]
    first_grad[...] = vec_in[0:TAPS, 0:SHARD]
    for at, ref in enumerate(vecs):
        ref[...] = vec_in[TAPS + at : TAPS + at + 1, 0:SHARD]
    for copy in stores:
        copy.wait()


def whole(shape):
    return pl.BlockSpec(shape, lambda i: (0,) * len(shape))


def local(
    waveforms, packing_list, segment_ids, first_weight, first_bias, first_gain, first_shift,
    second_weight, second_bias, second_gain, second_shift, cotangent,
):
    vecs = (first_bias, first_gain, first_shift, second_bias, second_gain, second_shift)
    vecs = [value.reshape(1, SHARD) for value in vecs]
    shape = jax.ShapeDtypeStruct
    dma = pltpu.SemaphoreType.DMA

    def block(i):
        return (0, jnp.clip(i - 1, 0, STEPS - 1), 0)

    def vmem(kind, *dims):
        return pltpu.VMEM(dims, kind)

    features, second_grad, vec_grad = pl.pallas_call(
        main_kernel,
        grid=(STEPS + 2,),
        out_shape=[shape((1, ROWS, CH), BF16), shape((SHARD, 3 * CH), F32), shape((16, 128), F32)],
        in_specs=[
            whole((4, 128)), whole((1, 128)), whole((320, FRAMES)), whole((TAPS, SHARD)),
            *([whole((1, SHARD))] * 6), whole((SHARD, 3 * CH)), pl.BlockSpec((1, TILE, CH), block),
        ],
        out_specs=[pl.BlockSpec((1, TILE, CH), block), whole((SHARD, 3 * CH)), whole((16, 128))],
        scratch_shapes=[
            vmem(BF16, 128, 320), vmem(BF16, 128, 320), vmem(BF16, 16, 128), vmem(BF16, 4, 16, 128),
            vmem(BF16, 16, 128), vmem(BF16, 4, 16, 128), vmem(BF16, 4, 4, SHARD, 3 * CH), vmem(F32, 144, 384),
            vmem(BF16, 128, CH), vmem(F32, 128, 256), vmem(BF16, TILE + 16, 384), vmem(BF16, 384, 384),
            vmem(BF16, STEPS, 2 * TILE, 128),
            vmem(F32, 16, CH), vmem(BF16, ROWS + 16, CH), vmem(BF16, ROWS, CH), vmem(BF16, ROWS, CH),
            vmem(BF16, ROWS, CH), vmem(BF16, ROWS, 128), vmem(BF16, ROWS, 128), vmem(BF16, ROWS, CH),
            vmem(BF16, ROWS, CH),
            vmem(F32, 8, CH), vmem(F32, CH, 3 * CH), vmem(F32, 24, CH), vmem(F32, TILE, CH), vmem(F32, TILE, CH),
            vmem(BF16, TILE, CH), vmem(BF16, TILE, CH), vmem(BF16, TILE, CH), vmem(BF16, TILE, CH),
            vmem(BF16, 4, 4, 2, 16, 3 * CH),
            vmem(F32, TILE, CH), vmem(F32, TILE, CH),
            vmem(BF16, 4, 4, 16, 3 * CH), vmem(BF16, 4, 4, 16, 3 * CH),
            vmem(BF16, 4, 4, 16, 768), vmem(BF16, 4, 4, 16, 768),
            vmem(BF16, 4, 16, 768), vmem(BF16, 4, 16, 768), vmem(BF16, 4, 16, 768), vmem(BF16, 4, 16, 768),
            vmem(F32, 16, 3 * CH), vmem(F32, 4, 16, 384), vmem(F32, 16, 384),
            vmem(F32, SHARD, 3 * CH), vmem(BF16, 128, CH), vmem(F32, 128, CH), vmem(F32, 128, 128),
            vmem(F32, 4, 16, 128), vmem(F32, 4, 16, 128), vmem(F32, 16, 128),
            vmem(F32, 4, 16, 128), vmem(F32, 16, 128), vmem(F32, DP, 16, 128),
            dma((DP,)), dma((DP,)), dma((4,)), dma((4,)), dma((4,)), dma((4,)),
            dma((2, 4)), dma((2, 4)), dma((2, 4)), dma((2, 4)), dma, dma,
            dma((4,)), dma((4,)), dma((2, 4)), dma((2, 4)), dma((2, 4)), dma((2, 4)),
            dma((4,)), dma((4,)), dma((DP,)), dma((DP,)),
            dma((4,)), dma((4,)), dma((4,)), dma((4,)), dma((DP,)), dma((DP,)),
        ],
        compiler_params=pltpu.CompilerParams(
            collective_id=0, has_side_effects=True, vmem_limit_bytes=VMEM_LIMIT
        ),
    )(packing_list, segment_ids, waveforms[0].T, first_weight.T, *vecs, second_weight, cotangent)

    one = shape((1, SHARD), F32)
    anywhere = pl.BlockSpec(memory_space=pl.ANY)
    local_vmem = pl.BlockSpec(memory_space=pltpu.VMEM)
    outs = pl.pallas_call(
        last_kernel,
        out_shape=[shape((1, ROWS, CH), BF16), shape((SHARD, 3 * CH), F32), shape((TAPS, SHARD), F32)] + [one] * 6,
        in_specs=[anywhere, local_vmem, local_vmem],
        out_specs=[anywhere] + [local_vmem] * 8,
        scratch_shapes=[pltpu.VMEM((1, ROWS, CH), BF16), dma((STEPS,)), dma((STEPS,))],
        compiler_params=pltpu.CompilerParams(vmem_limit_bytes=VMEM_LIMIT),
    )(features, second_grad, vec_grad)
    b1, n1, s1, b2, n2, s2 = [value.reshape(SHARD) for value in outs[3:]]
    return outs[0], outs[2].T, b1, n1, s1, outs[1], b2, n2, s2


def solution(mesh):
    placed = (
        P("dp", "fsdp", None), P(None, "fsdp"), P("dp", "fsdp"), P("fsdp", None), P("fsdp"), P("fsdp"),
        P("fsdp"), P("fsdp", None), P("fsdp"), P("fsdp"), P("fsdp"), P("dp", "fsdp", None),
    )
    out = (
        P("dp", "fsdp", None), P("fsdp", None), P("fsdp"), P("fsdp"), P("fsdp"), P("fsdp", None),
        P("fsdp"), P("fsdp"), P("fsdp"),
    )
    return jax.shard_map(local, mesh=mesh, in_specs=placed, out_specs=out, check_vma=False)
```
